32 devices in a mesh: lat: 8 (over z, y), depth: 4 (over x, core).
Axes of the slice: x: 2, y: 2, z: 4, core: 2. Of those that a mesh axis runs over, the one named last changes fastest.
Arguments:
- thermal_anomaly: float32 [128, 32, 2048], P('depth', 'lat'), may hold values from -6 to 6
- water_anomaly: float32 [128, 32, 2048], P('depth', 'lat'), may hold values from -6 to 6
- substrate_class_label: int32 [32, 2048], P('lat'), may hold values from 0 to 11
- sideways_thermal_spread: float32 [12], replicated, may hold values from 0.1 to 0.6
- sideways_water_factors: float32 [12], replicated, may hold values from 0.1 to 0.9
- thermal_solve_matrix: float32 [128, 128], replicated, may hold values from -0.3 to 1.3, as said below
- water_solve_matrix: float32 [128, 128], replicated, may hold values from -0.3 to 1.3, as said below
Outputs:
- temperature_next: float32 [128, 32, 2048], P('depth', 'lat')
- moisture_next: float32 [128, 32, 2048], P('depth', 'lat')
The draws below stay inside these ranges and needn't reach their ends.
Inputs may be any that keep to these rules, and one draw needn't show every extreme that they name: `thermal_solve_matrix`: a dense matrix with unit diagonal. `water_solve_matrix`: a dense matrix with unit diagonal.
All inputs are finite; a program needn't handle non-finite values.
Results may differ from the reference program's by a relative error of at most 0.00007.
Values sent between devices are 32-bit elements; how exact they have to be, the bound alone decides.
No kernel may reach another device: no remote copies, remote signals or barrier semaphores. Data moves between devices by JAX's collectives and lax.ppermute only.
A program may use at most 128 MiB of HBM per device.

```python
import math
import jax
import jax.numpy as jnp
from jax import lax

VERTICAL_POINTS = 128
CLASSES = 12
LSUB = 4
PLOTS_PER_LINE = 2048
MESH_LINES_TOTAL = 32


def solve_matrix(key):
    reach = 1.2 / VERTICAL_POINTS ** 0.5
    noise = jax.random.uniform(key, (VERTICAL_POINTS, VERTICAL_POINTS), jnp.float32, -reach, reach)
    diagonal = jnp.arange(VERTICAL_POINTS)[:, None] == jnp.arange(VERTICAL_POINTS)[None, :]
    return jnp.where(diagonal, 1.0, noise).astype(jnp.float32)


def draw_thermal_solve_matrix(key, part):
    return solve_matrix(jax.random.fold_in(key, 11))


def draw_water_solve_matrix(key, part):
    return solve_matrix(jax.random.fold_in(key, 23))


def plant(values, key, smallest, high):
    extent = values.shape
    index_at = [jax.random.randint(jax.random.fold_in(key, axis), (), 0, extent[axis]) for axis in range(len(extent))]
    values = values.at[tuple(index_at)].set(smallest)
    longest = extent.index(max(extent))
    index_at[longest] = (index_at[longest] + 1) % extent[longest]
    return values.at[tuple(index_at)].set(high)


def shard_levels(own_key, shape, pieces, smallest, high):
    loudness = 1.0
    for position, parts in pieces:
        heights = jax.random.uniform(jax.random.fold_in(jax.random.fold_in(own_key, 6), position), (parts,), jnp.float32, smallest / len(pieces), high / len(pieces))
        loudness = loudness * jnp.repeat(jnp.exp(heights), shape[position] // parts).reshape((-1,) + (1,) * (len(shape) - 1 - position))
    return loudness


def normal_values(own_key, shape, scale, bound, split=(), dtype=jnp.bfloat16):
    values = jax.random.normal(own_key, shape, jnp.float32) * scale
    if len(split) > 0:
        values = shard_levels(own_key, shape, split, -0.22, 0.18) * values
    return jnp.clip(values, min=-bound, max=bound).astype(dtype)


def setup_inputs(seed: int = 0) -> dict:
    key_of = jax.random.split(jax.random.key(seed), 8)
    return {
        "thermal_anomaly": normal_values(key_of[0], (VERTICAL_POINTS, MESH_LINES_TOTAL, PLOTS_PER_LINE), 1.0, 6.0, ((0, 4), (1, 8)), jnp.float32),
        "water_anomaly": normal_values(key_of[1], (VERTICAL_POINTS, MESH_LINES_TOTAL, PLOTS_PER_LINE), 1.0, 6.0, ((0, 4), (1, 8)), jnp.float32),
        "substrate_class_label": plant(jax.random.randint(key_of[2], (MESH_LINES_TOTAL, PLOTS_PER_LINE), 0, CLASSES), jax.random.fold_in(key_of[2], 1), 0, CLASSES - 1).astype(jnp.int32),
        "sideways_thermal_spread": jnp.clip(jnp.exp(jax.random.uniform(key_of[3], (CLASSES,), jnp.float32, math.log(0.1), math.log(0.6))), 0.1, 0.6),
        "sideways_water_factors": jnp.clip(jnp.exp(jax.random.uniform(key_of[4], (CLASSES,), jnp.float32, math.log(0.1), math.log(0.9))), 0.1, 0.9),
        "thermal_solve_matrix": draw_thermal_solve_matrix(jax.random.fold_in(key_of[7], 71), 0),
        "water_solve_matrix": draw_water_solve_matrix(jax.random.fold_in(key_of[7], 71), 0),
    }


RATE = 0.25


def cheb_matrix(count):
    index = jnp.arange(count).astype(jnp.float32)
    nodes = jnp.cos(jnp.pi * index / (count - 1))
    ends = jnp.where((index == 0) | (index == count - 1), 2.0, 1.0)
    signs = jnp.where(jnp.arange(count) % 2 == 0, 1.0, -1.0)
    weight = (ends * signs).astype(jnp.float32)
    diagonal = jnp.arange(count)[:, None] == jnp.arange(count)[None, :]
    spread = nodes[:, None] - nodes[None, :]
    off = weight[:, None] / weight[None, :] / jnp.where(diagonal, 1.0, spread)
    off = jnp.where(diagonal, 0.0, off)
    return off - jnp.diag(jnp.sum(off, axis=1)), nodes


def lateral_sum(after, before, centre):
    zeros = jnp.zeros_like(centre[..., :1])
    east = jnp.concatenate([centre[..., 1:], zeros], axis=-1)
    west = jnp.concatenate([zeros, centre[..., :-1]], axis=-1)
    return after + before + east + west - 4.0 * centre


def advance(profile_snapshot, lap, kappa_heat, kappa_moist):
    wet = profile_snapshot[1]
    kappa_t = kappa_heat * (1.0 + 0.5 * wet * wet / (1.0 + wet * wet))
    return jnp.stack([profile_snapshot[0] + RATE * kappa_t * lap[0], profile_snapshot[1] + RATE * kappa_moist * lap[1]])


def column_step(fields, deriv, nodes, thermal_solve_matrix, water_solve_matrix):
    high = lax.Precision.HIGHEST
    scale = (1.0 - nodes * nodes) / deriv.shape[0]
    drain = jnp.einsum("zk,k...->z...", deriv, fields[2], precision=high)
    drain = drain * scale.reshape((-1,) + (1,) * (fields.ndim - 2))
    rhs_heat = fields[0] - 0.25 * drain
    rhs_wet = fields[1] + 0.5 * drain
    new_heat = jnp.einsum("zk,k...->z...", thermal_solve_matrix, rhs_heat, precision=high)
    new_wet = jnp.einsum("zk,k...->z...", water_solve_matrix, rhs_wet, precision=high)
    return jnp.stack([new_heat, new_wet])


def reference(thermal_anomaly, water_anomaly, substrate_class_label, sideways_thermal_spread, sideways_water_factors, thermal_solve_matrix, water_solve_matrix):
    kappa_heat = sideways_thermal_spread[substrate_class_label]
    kappa_moist = sideways_water_factors[substrate_class_label]

    def vertical_level(pair):
        profile_snapshot = jnp.stack([pair[0], pair[1]])
        for step in range(LSUB):
            zeros = jnp.zeros_like(profile_snapshot[:, :1])
            after = jnp.concatenate([profile_snapshot[:, 1:], zeros], axis=1)
            before = jnp.concatenate([zeros, profile_snapshot[:, :-1]], axis=1)
            lap = lateral_sum(after, before, profile_snapshot)
            profile_snapshot = advance(profile_snapshot, lap, kappa_heat, kappa_moist)
        return profile_snapshot

    profile_snapshots = lax.map(vertical_level, (thermal_anomaly, water_anomaly))
    deriv, nodes = cheb_matrix(VERTICAL_POINTS)

    def row(item):
        heat_row, wet_row, kappa_row = item
        fields = jnp.stack([heat_row, wet_row, kappa_row[None, :] * wet_row])
        return column_step(fields, deriv, nodes, thermal_solve_matrix, water_solve_matrix)

    heat_rows = jnp.transpose(profile_snapshots[:, 0], (1, 0, 2))
    wet_rows = jnp.transpose(profile_snapshots[:, 1], (1, 0, 2))
    result = lax.map(row, (heat_rows, wet_rows, kappa_moist))
    return jnp.transpose(result[:, 0], (1, 0, 2)), jnp.transpose(result[:, 1], (1, 0, 2))
```

```python
import functools

import jax
import jax.numpy as jnp
import numpy as np
from jax import lax
from jax.experimental import pallas as pl
from jax.experimental.pallas import tpu as pltpu
from jax.sharding import PartitionSpec as P

DEPTH = 128
SLAB = 32
ROWS = 4
RATE = 0.25
CHUNKS = 2
JOINT = ("lat", "depth")
BODY = 2 * ROWS * SLAB
VMEM_LIMIT = 48 * 1024 * 1024


def params():
    return pltpu.CompilerParams(vmem_limit_bytes=VMEM_LIMIT)


def cost(flops, nbytes):
    return pl.CostEstimate(flops=flops, bytes_accessed=nbytes, transcendentals=0)


def scaled_cheb(count):
    f32 = np.float32
    index = np.arange(count).astype(f32)
    nodes = np.cos((f32(np.pi) * index / f32(count - 1)).astype(f32)).astype(f32)
    ends = np.where((index == 0) | (index == count - 1), 2.0, 1.0)
    signs = np.where(np.arange(count) % 2 == 0, 1.0, -1.0)
    weight = (ends * signs).astype(f32)
    diagonal = np.eye(count, dtype=bool)
    spread = nodes[:, None] - nodes[None, :]
    off = weight[:, None] / weight[None, :] / np.where(diagonal, f32(1.0), spread)
    off = np.where(diagonal, f32(0.0), off).astype(f32)
    deriv = off - np.diag(np.sum(off, axis=1, dtype=f32))
    scale = (f32(1.0) - nodes * nodes) / f32(count)
    return (scale[:, None] * deriv).astype(f32)


def place():
    lat = lax.axis_index("lat")
    dep = lax.axis_index("depth")
    return lax.rem(lat, 2), lax.div(dep, 2), lax.rem(dep, 2)


def quarter():
    y, x, _ = place()
    return 2 * y + x


def column_start(k, mask, width):
    return pl.multiple_of((lax.bitwise_xor(quarter(), mask) * CHUNKS + k) * width, 128)


def lanes(shape):
    return lax.broadcasted_iota(jnp.int32, shape, len(shape) - 1)


def pack_kernel(k, width, heat_ref, wet_ref, label_ref, *blocks):
    columns = heat_ref.shape[2]
    lane = lanes((SLAB, 128))
    lane8 = lanes((8, 128))
    lane4 = lanes((ROWS, 128))
    for mask in range(4):
        start = column_start(k, mask, width)
        left = pl.multiple_of(jnp.maximum(start - 128, 0), 128)
        right = pl.multiple_of(jnp.minimum(start + width, columns - 128), 128)
        keep_left = (start > 0).astype(jnp.float32)
        keep_right = (start + width < columns).astype(jnp.float32)
        for f, ref in enumerate((heat_ref, wet_ref)):
            packed = jnp.zeros((8, 128), jnp.float32)
            for r in range(ROWS):
                base = (f * ROWS + r) * SLAB
                blocks[mask][base : base + SLAB, :] = ref[:, r, pl.ds(start, width)]
                edge = jnp.where(
                    lane >= 64,
                    ref[:, r, pl.ds(left, 128)] * keep_left,
                    ref[:, r, pl.ds(right, 128)] * keep_right,
                )
                for g in range(SLAB // 8):
                    at = 8 * (r * (SLAB // 8) + g)
                    moved = pltpu.roll(edge[8 * g : 8 * g + 8], (at + 4) % 128, 1)
                    packed = jnp.where((lane8 >= at) & (lane8 < at + 8), moved, packed)
            blocks[mask][BODY : BODY + 8, 128 * f : 128 * f + 128] = packed
        blocks[mask][BODY + 8 : BODY + 12, :] = (
            label_ref[:, pl.ds(start, width)] + 1
        ).astype(jnp.float32)
        edge = jnp.where(
            lane4 >= 124,
            (label_ref[:, pl.ds(left, 128)] + 1).astype(jnp.float32) * keep_left,
            (label_ref[:, pl.ds(right, 128)] + 1).astype(jnp.float32) * keep_right,
        )
        blocks[mask][BODY + 12 : BODY + 16, :] = jnp.zeros((ROWS, width), jnp.float32)
        blocks[mask][BODY + 12 : BODY + 16, :128] = jnp.where(
            (lane4 >= 124) | (lane4 < 4), edge, 0.0
        )


def pack(k, width, heat, wet, label):
    shape = jax.ShapeDtypeStruct((BODY + 16, width), jnp.float32)
    return pl.pallas_call(
        functools.partial(pack_kernel, k, width),
        out_shape=[shape] * 4,
        in_specs=[pl.BlockSpec(memory_space=pltpu.VMEM)] * 3,
        out_specs=[pl.BlockSpec(memory_space=pltpu.VMEM)] * 4,
        compiler_params=params(),
        cost_estimate=cost(0, 4 << 20),
        name="pack",
    )(heat, wet, label)


def prep_kernel(thermal_ref, water_ref, cheb_ref, stack_w_ref, stack_h_ref):
    _, x, c = place()
    dot = functools.partial(
        jnp.dot, precision=lax.Precision.HIGHEST, preferred_element_type=jnp.float32
    )

    def depth_of(n):
        slab, inner = lax.div(n, SLAB), lax.rem(n, SLAB)
        dx = lax.rem(slab, 2)
        dc = lax.div(slab, 2)
        return (2 * lax.rem(x + dx, 2) + lax.rem(c + dc, 2)) * SLAB + inner

    row = lax.broadcasted_iota(jnp.int32, (DEPTH, DEPTH), 0)
    col = lax.broadcasted_iota(jnp.int32, (DEPTH, DEPTH), 1)
    order = (row == depth_of(col)).astype(jnp.float32)
    picks = (depth_of(row[: 2 * SLAB]) == col[: 2 * SLAB]).astype(jnp.float32)
    thermal = dot(picks, thermal_ref[...])
    water = dot(picks, water_ref[...])
    cheb = cheb_ref[...]
    stack_w = jnp.concatenate(
        [water, -0.25 * dot(thermal, cheb), 0.5 * dot(water, cheb)], axis=0
    )
    for ref, stack in ((stack_w_ref, stack_w), (stack_h_ref, thermal)):
        ordered = dot(stack, order)
        high = ordered.astype(jnp.bfloat16)
        low = (ordered - high.astype(jnp.float32)).astype(jnp.bfloat16)
        count = ordered.shape[0]
        ref[:count, :] = high
        ref[count:, :] = low


def prep(thermal, water):
    cheb = jnp.asarray(scaled_cheb(DEPTH))
    return pl.pallas_call(
        prep_kernel,
        out_shape=[
            jax.ShapeDtypeStruct((12 * SLAB, DEPTH), jnp.bfloat16),
            jax.ShapeDtypeStruct((4 * SLAB, DEPTH), jnp.bfloat16),
        ],
        in_specs=[pl.BlockSpec(memory_space=pltpu.VMEM)] * 3,
        out_specs=[pl.BlockSpec(memory_space=pltpu.VMEM)] * 2,
        compiler_params=params(),
        cost_estimate=cost(1 << 24, 1 << 18),
        name="prep",
    )(thermal, water, cheb)


def substep(above, here, below, kappa_heat, kappa_moist):
    laps = []
    size = here[0].shape[1]
    for f in range(2):
        u = here[f]
        sides = pltpu.roll(u, 1, 1) + pltpu.roll(u, size - 1, 1)
        laps.append((above[f] + below[f]) + sides - 4.0 * u)
    heat, wet = here
    body = 1.0 + wet * wet
    guess = pl.reciprocal(body, approx=True)
    inverse = guess * (2.0 - body * guess)
    spread = kappa_heat * (1.5 - 0.5 * inverse)
    return heat + spread * laps[0], wet + kappa_moist * laps[1]


def factors(label, spread_ref, factor_ref):
    heat = jnp.zeros(label.shape, jnp.float32)
    moist = jnp.zeros(label.shape, jnp.float32)
    for i in range(spread_ref.shape[0]):
        here = label == i + 1.0
        heat = jnp.where(here, spread_ref[i], heat)
        moist = jnp.where(here, factor_ref[i], moist)
    return heat, moist


def stencil_kernel(
    width, own, rx, ry, rxy, p1, p2, spread_ref, factor_ref, post, km_ref, kap
):
    y, _, _ = place()
    count = 4 * ROWS
    for j, block in enumerate((p2.at[0], own, ry, p1.at[0])):
        label = block[BODY + 8 : BODY + 16, :]
        body = factors(label[:ROWS], spread_ref, factor_ref)
        edge = factors(label[ROWS:, :128], spread_ref, factor_ref)
        if 1 <= j < 3:
            km_ref[(j - 1) * ROWS : j * ROWS, :] = body[1]
        for f in range(2):
            whole = RATE * jnp.concatenate([body[f], edge[f]], axis=1)
            back = jnp.concatenate(
                [whole[r : r + 1] for r in reversed(range(ROWS))], axis=0
            )
            kap[f, j * ROWS : j * ROWS + ROWS, :] = jnp.where(y == 1, back, whole)

    def stored(r):
        return jnp.where(y == 1, ROWS - 1 - r, r)

    for s in range(2):
        blocks = (p2.at[s], (own, rx)[s], (ry, rxy)[s], p1.at[s])

        def group(g, carry):
            def load(j):
                block, r = blocks[j // ROWS], stored(j % ROWS)
                shift = lax.rem(252 - 8 * (r * (SLAB // 8) + g), 128)
                fields = []
                for f in range(2):
                    at = pl.multiple_of((f * ROWS + r) * SLAB + 8 * g, 8)
                    edge = pltpu.roll(
                        block[BODY : BODY + 8, 128 * f : 128 * f + 128], shift, 1
                    )
                    fields.append(jnp.concatenate([block[pl.ds(at, 8), :], edge], axis=1))
                return tuple(fields)

            levels = [dict() for _ in range(5)]
            for j in range(count + 4):
                if j < count:
                    levels[0][j] = load(j)
                for t in range(1, 5):
                    i = j - t
                    if t <= i < count - t:
                        prev = levels[t - 1]
                        levels[t][i] = substep(
                            prev[i - 1],
                            prev[i],
                            prev[i + 1],
                            kap[0, i : i + 1, :],
                            kap[1, i : i + 1, :],
                        )
                        if t == 4:
                            strip, r = divmod(i - ROWS, ROWS)
                            for f in range(2):
                                post[
                                    f,
                                    strip * ROWS + stored(r),
                                    pl.ds(pl.multiple_of(s * SLAB + 8 * g, 8), 8),
                                    :,
                                ] = levels[4][i][f][:, :width]
            return carry

        lax.fori_loop(0, SLAB // 8, group, 0)


def stencil(width, own, rx, ry, rxy, p1, p2, spread, factor):
    return pl.pallas_call(
        functools.partial(stencil_kernel, width),
        out_shape=[
            jax.ShapeDtypeStruct((2, 2 * ROWS, 2 * SLAB, width), jnp.float32),
            jax.ShapeDtypeStruct((2 * ROWS, width), jnp.float32),
        ],
        in_specs=[pl.BlockSpec(memory_space=pltpu.VMEM)] * 6
        + [pl.BlockSpec(memory_space=pltpu.SMEM)] * 2,
        out_specs=[pl.BlockSpec(memory_space=pltpu.VMEM)] * 2,
        scratch_shapes=[pltpu.VMEM((2, 4 * ROWS, width + 128), jnp.float32)],
        compiler_params=params(),
        cost_estimate=cost(1 << 24, 4 << 20),
        name="stencil",
    )(own, rx, ry, rxy, p1, p2, spread, factor)


def split(values):
    high = values.astype(jnp.bfloat16)
    return high, (values - high.astype(jnp.float32)).astype(jnp.bfloat16)


def solve_kernel(mine, other, stack_w, stack_h, km, *blocks):
    dot = functools.partial(jnp.dot, preferred_element_type=jnp.float32)
    half = 2 * SLAB

    def apply(stack, values):
        high, low = split(values)
        count = stack.shape[0] // 2
        both = dot(stack[...], high)
        return both[:count] + both[count:] + dot(stack[:count, :], low)

    for r in range(2 * ROWS):
        heat = apply(stack_h, jnp.concatenate([mine[0, r], other[0, r]], axis=0))
        wet = apply(stack_w, jnp.concatenate([mine[1, r], other[1, r]], axis=0))
        factor = km[r : r + 1, :]
        results = (
            heat + factor * wet[half : 2 * half],
            wet[:half] + factor * wet[2 * half :],
        )
        strip, inner = divmod(r, ROWS)
        for f in range(2):
            base = (f * ROWS + inner) * SLAB
            for slab in range(2):
                blocks[2 * strip + slab][base : base + SLAB, :] = results[f][
                    slab * SLAB : slab * SLAB + SLAB
                ]


def solve(width, mine, other, stack_w, stack_h, km):
    shape = jax.ShapeDtypeStruct((BODY, width), jnp.float32)
    return pl.pallas_call(
        solve_kernel,
        out_shape=[shape] * 4,
        in_specs=[pl.BlockSpec(memory_space=pltpu.VMEM)] * 5,
        out_specs=[pl.BlockSpec(memory_space=pltpu.VMEM)] * 4,
        compiler_params=params(),
        cost_estimate=cost(1 << 26, 4 << 20),
        name="solve",
    )(mine, other, stack_w, stack_h, km)


def assemble_kernel(width, *refs):
    blocks, outs = refs[:-2], refs[-2:]
    for k in range(CHUNKS):
        for mask in range(4):
            start = column_start(k, mask, width)
            for f in range(2):
                for r in range(ROWS):
                    base = (f * ROWS + r) * SLAB
                    outs[f][:, r, pl.ds(start, width)] = blocks[4 * k + mask][
                        base : base + SLAB, :
                    ]


def assemble(width, columns, blocks):
    shape = jax.ShapeDtypeStruct((SLAB, ROWS, columns), jnp.float32)
    return pl.pallas_call(
        functools.partial(assemble_kernel, width),
        out_shape=[shape] * 2,
        in_specs=[pl.BlockSpec(memory_space=pltpu.VMEM)] * len(blocks),
        out_specs=[pl.BlockSpec(memory_space=pltpu.VMEM)] * 2,
        compiler_params=params(),
        cost_estimate=cost(0, 4 << 20),
        name="assemble",
    )(*blocks)


def routes(strips):
    cells = [(l, d) for l in range(strips) for d in range(4)]

    def pairs(to):
        return [
            (l * 4 + d, to(l, d)[0] * 4 + to(l, d)[1])
            for l, d in cells
            if 0 <= to(l, d)[0] < strips
        ]

    return {
        "x": pairs(lambda l, d: (l, d ^ 2)),
        "y": pairs(lambda l, d: (l ^ 1, d)),
        "xy": pairs(lambda l, d: (l ^ 1, d ^ 2)),
        "core": pairs(lambda l, d: (l, d ^ 1)),
        "own": pairs(lambda l, d: (l + 2 if l % 2 else l - 2, d)),
        "partner": pairs(lambda l, d: (l - 2 if l % 2 else l + 2, d)),
    }


def per_device(strips, heat, wet, label, spread, factor, thermal, water):
    columns = heat.shape[2]
    width = columns // (4 * CHUNKS)
    route = routes(strips)

    def send(array, name):
        return lax.ppermute(array, JOINT, route[name])

    received = []
    for k in range(CHUNKS):
        own, bx, by, bxy = pack(k, width, heat, wet, label)
        received.append((own, send(bx, "x"), send(by, "y"), send(bxy, "xy")))
    stack_w, stack_h = prep(thermal, water)
    blocks = []
    for k in range(CHUNKS):
        own, rx, ry, rxy = received[k]
        p1 = send(jnp.stack([own, rx]), "own")
        p2 = send(jnp.stack([ry, rxy]), "partner")
        post, km = stencil(width, own, rx, ry, rxy, p1, p2, spread, factor)
        other = send(post, "core")
        kept, bx, by, bxy = solve(width, post, other, stack_w, stack_h, km)
        blocks += [kept, send(bx, "x"), send(by, "y"), send(bxy, "xy")]
    return tuple(assemble(width, columns, blocks))


def solution(mesh):
    return jax.shard_map(
        functools.partial(per_device, mesh.shape["lat"]),
        mesh=mesh,
        in_specs=(
            P("depth", "lat", None),
            P("depth", "lat", None),
            P("lat", None),
            P(),
            P(),
            P(),
            P(),
        ),
        out_specs=(P("depth", "lat", None), P("depth", "lat", None)),
        check_vma=False,
    )
```

```python
import functools

import jax
import jax.numpy as jnp
import numpy as np
from jax import lax
from jax.experimental import pallas as pl
from jax.experimental.pallas import tpu as pltpu
from jax.sharding import PartitionSpec as P

DEPTH = 128
SLAB = 32
ROWS = 4
RATE = 0.25
PARTS = (2, 2)
JOINT = ("lat", "depth")
BODY = 2 * ROWS * SLAB
VMEM_LIMIT = 48 * 1024 * 1024
FIRST_LIMIT = 62 * 1024 * 1024


def params(limit=VMEM_LIMIT):
    return pltpu.CompilerParams(vmem_limit_bytes=limit)


def cost(flops, nbytes):
    return pl.CostEstimate(flops=0, bytes_accessed=1024, transcendentals=0)


def scaled_cheb(count):
    f32 = np.float32
    index = np.arange(count).astype(f32)
    nodes = np.cos((f32(np.pi) * index / f32(count - 1)).astype(f32)).astype(f32)
    ends = np.where((index == 0) | (index == count - 1), 2.0, 1.0)
    signs = np.where(np.arange(count) % 2 == 0, 1.0, -1.0)
    weight = (ends * signs).astype(f32)
    diagonal = np.eye(count, dtype=bool)
    spread = nodes[:, None] - nodes[None, :]
    off = weight[:, None] / weight[None, :] / np.where(diagonal, f32(1.0), spread)
    off = np.where(diagonal, f32(0.0), off).astype(f32)
    deriv = off - np.diag(np.sum(off, axis=1, dtype=f32))
    scale = (f32(1.0) - nodes * nodes) / f32(count)
    return (scale[:, None] * deriv).astype(f32)


def place():
    lat = lax.axis_index("lat")
    dep = lax.axis_index("depth")
    return lax.rem(lat, 2), lax.div(dep, 2), lax.rem(dep, 2)


def quarter():
    y, x, _ = place()
    return 2 * y + x


def chunk_width(k, columns):
    return columns * PARTS[k] // (4 * sum(PARTS))


def column_start(k, mask, columns):
    offset = sum(chunk_width(i, columns) for i in range(k))
    return pl.multiple_of(
        lax.bitwise_xor(quarter(), mask) * (columns // 4) + offset, 128
    )


def halo_at(f, width):
    return (BODY, 128 * f) if width >= 256 else (BODY + 8 * f, 0)


def label_at(width):
    return BODY + (8 if width >= 256 else 16)


def block_rows(width):
    return label_at(width) + 8


def lanes(shape):
    return lax.broadcasted_iota(jnp.int32, shape, len(shape) - 1)


def pack_kernel(k, width, heat_hbm, wet_hbm, label_hbm, *refs):
    *blocks, near, label_ref, sems = refs
    columns = heat_hbm.shape[2]
    window = near.shape[4]
    labels = pltpu.make_async_copy(label_hbm, label_ref, sems.at[8])
    labels.start()
    bases, copies = [], []
    for mask in (1, 2, 3, 0):
        start = column_start(k, mask, columns)
        base = pl.multiple_of(jnp.clip(start - 128, 0, columns - window), 128)
        pair = [
            pltpu.make_async_copy(
                far.at[:, :, pl.ds(base, window)], near.at[mask, f], sems.at[2 * mask + f]
            )
            for f, far in enumerate((heat_hbm, wet_hbm))
        ]
        for copy in pair:
            copy.start()
        bases.append(base)
        copies.append(pair)
    labels.wait()
    lane = lanes((SLAB, 128))
    lane8 = lanes((8, 128))
    lane4 = lanes((ROWS, 128))
    for mask, base, pair in zip((1, 2, 3, 0), bases, copies):
        for copy in pair:
            copy.wait()
        start = column_start(k, mask, columns)
        left = pl.multiple_of(jnp.maximum(start - 128, 0), 128)
        right = pl.multiple_of(jnp.minimum(start + width, columns - 128), 128)
        keep_left = (start > 0).astype(jnp.float32)
        keep_right = (start + width < columns).astype(jnp.float32)
        main, before, after = (pl.multiple_of(at - base, 128) for at in (start, left, right))
        for f in range(2):
            ref = near.at[mask, f]
            packed = jnp.zeros((8, 128), jnp.float32)
            for r in range(ROWS):
                row = (f * ROWS + r) * SLAB
                blocks[mask][row : row + SLAB, :] = ref[:, r, pl.ds(main, width)]
                edge = jnp.where(
                    lane >= 64,
                    ref[:, r, pl.ds(before, 128)] * keep_left,
                    ref[:, r, pl.ds(after, 128)] * keep_right,
                )
                for g in range(SLAB // 8):
                    at = 8 * (r * (SLAB // 8) + g)
                    moved = pltpu.roll(edge[8 * g : 8 * g + 8], (at + 4) % 128, 1)
                    packed = jnp.where((lane8 >= at) & (lane8 < at + 8), moved, packed)
            at, lane_at = halo_at(f, width)
            blocks[mask][at : at + 8, lane_at : lane_at + 128] = packed
        types = label_at(width)
        blocks[mask][types : types + 4, :] = (
            label_ref[:, pl.ds(start, width)] + 1
        ).astype(jnp.float32)
        edge = jnp.where(
            lane4 >= 124,
            (label_ref[:, pl.ds(left, 128)] + 1).astype(jnp.float32) * keep_left,
            (label_ref[:, pl.ds(right, 128)] + 1).astype(jnp.float32) * keep_right,
        )
        blocks[mask][types + 4 : types + 8, :] = jnp.zeros((ROWS, width), jnp.float32)
        blocks[mask][types + 4 : types + 8, :128] = jnp.where(
            (lane4 >= 124) | (lane4 < 4), edge, 0.0
        )


def pack(k, width, heat, wet, label):
    shape = jax.ShapeDtypeStruct((block_rows(width), width), jnp.float32)
    return pl.pallas_call(
        functools.partial(pack_kernel, k, width),
        out_shape=[shape] * 4,
        in_specs=[pl.BlockSpec(memory_space=pltpu.HBM)] * 3,
        out_specs=[pl.BlockSpec(memory_space=pltpu.VMEM)] * 4,
        scratch_shapes=[
            pltpu.VMEM((4, 2, SLAB, ROWS, min(width + 256, heat.shape[2])), jnp.float32),
            pltpu.VMEM(label.shape, jnp.int32),
            pltpu.SemaphoreType.DMA((9,)),
        ],
        compiler_params=params(VMEM_LIMIT if k else FIRST_LIMIT),
        cost_estimate=cost(0, 4 << 20),
        name="pack",
    )(heat, wet, label)


def prep_kernel(thermal_ref, water_ref, cheb_ref, stack_w_ref, stack_h_ref):
    _, x, c = place()
    dot = functools.partial(
        jnp.dot, precision=lax.Precision.HIGHEST, preferred_element_type=jnp.float32
    )

    def depth_of(n):
        slab, inner = lax.div(n, SLAB), lax.rem(n, SLAB)
        dx = lax.rem(slab, 2)
        dc = lax.div(slab, 2)
        return (2 * lax.rem(x + dx, 2) + lax.rem(c + dc, 2)) * SLAB + inner

    row = lax.broadcasted_iota(jnp.int32, (DEPTH, DEPTH), 0)
    col = lax.broadcasted_iota(jnp.int32, (DEPTH, DEPTH), 1)
    order = (row == depth_of(col)).astype(jnp.float32)
    picks = (depth_of(row[: 2 * SLAB]) == col[: 2 * SLAB]).astype(jnp.float32)
    thermal = dot(picks, thermal_ref[...])
    water = dot(picks, water_ref[...])
    cheb = cheb_ref[...]
    stack_w = jnp.concatenate(
        [water, -0.25 * dot(thermal, cheb), 0.5 * dot(water, cheb)], axis=0
    )
    for ref, stack in ((stack_w_ref, stack_w), (stack_h_ref, thermal)):
        ordered = dot(stack, order)
        high = ordered.astype(jnp.bfloat16)
        low = (ordered - high.astype(jnp.float32)).astype(jnp.bfloat16)
        count = ordered.shape[0]
        ref[:count, :] = high
        ref[count:, :] = low


def prep(thermal, water):
    cheb = jnp.asarray(scaled_cheb(DEPTH))
    return pl.pallas_call(
        prep_kernel,
        out_shape=[
            jax.ShapeDtypeStruct((12 * SLAB, DEPTH), jnp.bfloat16),
            jax.ShapeDtypeStruct((4 * SLAB, DEPTH), jnp.bfloat16),
        ],
        in_specs=[pl.BlockSpec(memory_space=pltpu.VMEM)] * 3,
        out_specs=[pl.BlockSpec(memory_space=pltpu.VMEM)] * 2,
        compiler_params=params(),
        cost_estimate=cost(1 << 24, 1 << 18),
        name="prep",
    )(thermal, water, cheb)


def substep(above, here, below, kappa_heat, kappa_moist):
    laps = []
    size = here[0].shape[1]
    for f in range(2):
        u = here[f]
        sides = pltpu.roll(u, 1, 1) + pltpu.roll(u, size - 1, 1)
        laps.append((above[f] + below[f]) + sides - 4.0 * u)
    heat, wet = here
    body = 1.0 + wet * wet
    guess = pl.reciprocal(body, approx=True)
    inverse = guess * (2.0 - body * guess)
    spread = kappa_heat * (1.5 - 0.5 * inverse)
    return heat + spread * laps[0], wet + kappa_moist * laps[1]


def factors(label, spread_ref, factor_ref):
    heat = jnp.zeros(label.shape, jnp.float32)
    moist = jnp.zeros(label.shape, jnp.float32)
    for i in range(spread_ref.shape[0]):
        here = label == i + 1.0
        heat = jnp.where(here, spread_ref[i], heat)
        moist = jnp.where(here, factor_ref[i], moist)
    return heat, moist


INNER = [(1, 5), (1, 6), (1, 9), (1, 10), (2, 6), (2, 7), (2, 8), (2, 9), (3, 7), (3, 8)]
COUNT = 4 * ROWS


def stored(r):
    return jnp.where(lax.rem(lax.axis_index("lat"), 2) == 1, ROWS - 1 - r, r)


def strip_factors(width, block, spread_ref, factor_ref):
    y, _, _ = place()
    label = block[label_at(width) : label_at(width) + 8, :]
    body = factors(label[:ROWS], spread_ref, factor_ref)
    edge = factors(label[ROWS:, :128], spread_ref, factor_ref)
    for f in range(2):
        whole = jnp.concatenate([body[f], edge[f]], axis=1)
        back = jnp.concatenate([whole[r : r + 1] for r in reversed(range(ROWS))], axis=0)
        yield jnp.where(y == 1, back, whole)


def load_row(width, block, r, g):
    r = stored(r)
    shift = lax.rem(252 - 8 * (r * (SLAB // 8) + g), 128)
    fields = []
    for f in range(2):
        at = pl.multiple_of((f * ROWS + r) * SLAB + 8 * g, 8)
        row, lane = halo_at(f, width)
        edge = pltpu.roll(block[row : row + 8, lane : lane + 128], shift, 1)
        fields.append(jnp.concatenate([block[pl.ds(at, 8), :], edge], axis=1))
    return tuple(fields)


def pre_kernel(width, own, rx, ry, rxy, spread_ref, factor_ref, _, inner, kap, km_ref):
    for j, block in enumerate((own, ry)):
        to = slice(j * ROWS, j * ROWS + ROWS)
        for f, whole in enumerate(strip_factors(width, block, spread_ref, factor_ref)):
            kap[f, to, :] = RATE * whole
            if f == 1:
                km_ref[to, :] = factors(block[label_at(width) : label_at(width) + ROWS, :], spread_ref, factor_ref)[1]
    for s in range(2):
        blocks = ((own, rx)[s], (ry, rxy)[s])

        def group(g, carry):
            levels = [dict() for _ in range(4)]
            at = pl.ds(pl.multiple_of(s * SLAB + 8 * g, 8), 8)
            for j in range(ROWS, 3 * ROWS + 3):
                if j < 3 * ROWS:
                    levels[0][j] = load_row(width, blocks[j // ROWS - 1], j % ROWS, g)
                for t in range(1, 4):
                    i = j - t
                    if ROWS + t <= i < 3 * ROWS - t:
                        prev, k = levels[t - 1], i - ROWS
                        levels[t][i] = substep(
                            prev[i - 1], prev[i], prev[i + 1], kap[0, k : k + 1, :], kap[1, k : k + 1, :]
                        )
                        if (t, i) in INNER:
                            for f in range(2):
                                inner[INNER.index((t, i)), f, at, :] = levels[t][i][f]
            return carry

        lax.fori_loop(0, SLAB // 8, group, 0)


def pre(width, own, rx, ry, rxy, spread, factor, after):
    wide = width + 128
    return pl.pallas_call(
        functools.partial(pre_kernel, width),
        out_shape=[
            jax.ShapeDtypeStruct((len(INNER), 2, 2 * SLAB, wide), jnp.float32),
            jax.ShapeDtypeStruct((2, 2 * ROWS, wide), jnp.float32),
            jax.ShapeDtypeStruct((2 * ROWS, width), jnp.float32),
        ],
        in_specs=[pl.BlockSpec(memory_space=pltpu.VMEM)] * 4
        + [pl.BlockSpec(memory_space=pltpu.SMEM)] * 2
        + [pl.BlockSpec(memory_space=pl.ANY)],
        out_specs=[pl.BlockSpec(memory_space=pltpu.VMEM)] * 3,
        compiler_params=params(),
        cost_estimate=cost(1 << 24, 4 << 20),
        name="inner_substeps",
    )(own, rx, ry, rxy, spread, factor, after)


def stencil_kernel(
    width, own, rx, ry, rxy, p1, p2, inner, kap_ref, spread_ref, factor_ref, _, post, kap
):
    kap[:, ROWS : 3 * ROWS, :] = kap_ref[...]
    for j, block in ((0, p2.at[0]), (3, p1.at[0])):
        for f, whole in enumerate(strip_factors(width, block, spread_ref, factor_ref)):
            kap[f, j * ROWS : j * ROWS + ROWS, :] = RATE * whole
    for s in range(2):
        blocks = (p2.at[s], (own, rx)[s], (ry, rxy)[s], p1.at[s])

        def group(g, carry):
            at = pl.ds(pl.multiple_of(s * SLAB + 8 * g, 8), 8)
            levels = [dict() for _ in range(5)]
            for j in range(COUNT + 4):
                if j < COUNT and not ROWS + 2 <= j < 3 * ROWS - 2:
                    levels[0][j] = load_row(width, blocks[j // ROWS], j % ROWS, g)
                for t in range(1, 5):
                    i = j - t
                    if (t, i) in INNER:
                        k = INNER.index((t, i))
                        levels[t][i] = tuple(inner[k, f, at, :] for f in range(2))
                    elif t <= i < COUNT - t and not (t < 4 and ROWS + t <= i < 3 * ROWS - t):
                        prev = levels[t - 1]
                        levels[t][i] = substep(
                            prev[i - 1], prev[i], prev[i + 1], kap[0, i : i + 1, :], kap[1, i : i + 1, :]
                        )
                        if t == 4:
                            row = (i - ROWS) // ROWS * ROWS + stored(i % ROWS)
                            for f in range(2):
                                post[f, row, at, :] = levels[4][i][f][:, :width]
            return carry

        lax.fori_loop(0, SLAB // 8, group, 0)


def stencil(width, own, rx, ry, rxy, p1, p2, inner, kap, spread, factor, after):
    return pl.pallas_call(
        functools.partial(stencil_kernel, width),
        out_shape=jax.ShapeDtypeStruct((2, 2 * ROWS, 2 * SLAB, width), jnp.float32),
        in_specs=[pl.BlockSpec(memory_space=pltpu.VMEM)] * 8
        + [pl.BlockSpec(memory_space=pltpu.SMEM)] * 2
        + [pl.BlockSpec(memory_space=pl.ANY)],
        out_specs=pl.BlockSpec(memory_space=pltpu.VMEM),
        scratch_shapes=[pltpu.VMEM((2, COUNT, width + 128), jnp.float32)],
        compiler_params=params(),
        cost_estimate=cost(1 << 24, 4 << 20),
        name="outer_substeps",
    )(own, rx, ry, rxy, p1, p2, inner, kap, spread, factor, after)


def split(values):
    high = values.astype(jnp.bfloat16)
    return high, (values - high.astype(jnp.float32)).astype(jnp.bfloat16)


def solve_kernel(mine, other, stack_w, stack_h, km, *blocks):
    dot = functools.partial(jnp.dot, preferred_element_type=jnp.float32)
    half = 2 * SLAB

    def apply(stack, values):
        high, low = split(values)
        count = stack.shape[0] // 2
        both = dot(stack[...], high)
        return both[:count] + both[count:] + dot(stack[:count, :], low)

    for r in range(2 * ROWS):
        heat = apply(stack_h, jnp.concatenate([mine[0, r], other[0, r]], axis=0))
        wet = apply(stack_w, jnp.concatenate([mine[1, r], other[1, r]], axis=0))
        factor = km[r : r + 1, :]
        results = (
            heat + factor * wet[half : 2 * half],
            wet[:half] + factor * wet[2 * half :],
        )
        strip, inner = divmod(r, ROWS)
        for f in range(2):
            base = (f * ROWS + inner) * SLAB
            for slab in range(2):
                blocks[2 * strip + slab][base : base + SLAB, :] = results[f][
                    slab * SLAB : slab * SLAB + SLAB
                ]


def solve(width, mine, other, stack_w, stack_h, km):
    shape = jax.ShapeDtypeStruct((BODY, width), jnp.float32)
    return pl.pallas_call(
        solve_kernel,
        out_shape=[shape] * 4,
        in_specs=[pl.BlockSpec(memory_space=pltpu.VMEM)] * 5,
        out_specs=[pl.BlockSpec(memory_space=pltpu.VMEM)] * 4,
        compiler_params=params(),
        cost_estimate=cost(1 << 26, 4 << 20),
        name="solve",
    )(mine, other, stack_w, stack_h, km)


def assemble_kernel(k, width, *refs):
    blocks, outs, scratch, sems = refs[:4], refs[-4:-2], refs[-2], refs[-1]
    columns = outs[0].shape[2]
    copies = []
    for mask in range(4):
        start = column_start(k, mask, columns)
        for f in range(2):
            for r in range(ROWS):
                base = (f * ROWS + r) * SLAB
                scratch[mask, f, :, r, :] = blocks[mask][base : base + SLAB, :]
            copy = pltpu.make_async_copy(
                scratch.at[mask, f],
                outs[f].at[:, :, pl.ds(start, width)],
                sems.at[2 * mask + f],
            )
            copy.start()
            copies.append(copy)
    for copy in copies:
        copy.wait()


def assemble(k, width, columns, blocks, outs):
    shape = jax.ShapeDtypeStruct((SLAB, ROWS, columns), jnp.float32)
    return pl.pallas_call(
        functools.partial(assemble_kernel, k, width),
        out_shape=[shape] * 2,
        in_specs=[pl.BlockSpec(memory_space=pltpu.VMEM)] * 4
        + [pl.BlockSpec(memory_space=pltpu.HBM)] * len(outs),
        out_specs=[pl.BlockSpec(memory_space=pltpu.HBM)] * 2,
        scratch_shapes=[
            pltpu.VMEM((4, 2, SLAB, ROWS, width), jnp.float32),
            pltpu.SemaphoreType.DMA((8,)),
        ],
        input_output_aliases={4 + i: i for i in range(len(outs))},
        compiler_params=params(),
        cost_estimate=cost(0, 4 << 20),
        name="assemble",
    )(*blocks, *outs)


def routes(strips):
    cells = [(l, d) for l in range(strips) for d in range(4)]

    def pairs(to):
        return [
            (l * 4 + d, to(l, d)[0] * 4 + to(l, d)[1])
            for l, d in cells
            if 0 <= to(l, d)[0] < strips
        ]

    return {
        "x": pairs(lambda l, d: (l, d ^ 2)),
        "y": pairs(lambda l, d: (l ^ 1, d)),
        "xy": pairs(lambda l, d: (l ^ 1, d ^ 2)),
        "core": pairs(lambda l, d: (l, d ^ 1)),
        "own": pairs(lambda l, d: (l + 2 if l % 2 else l - 2, d)),
        "partner": pairs(lambda l, d: (l - 2 if l % 2 else l + 2, d)),
    }


def per_device(strips, heat, wet, label, spread, factor, thermal, water):
    columns = heat.shape[2]
    widths = [chunk_width(k, columns) for k in range(len(PARTS))]
    route = routes(strips)

    def send(array, name):
        return lax.ppermute(array, JOINT, route[name])

    received = []
    for k, width in enumerate(widths):
        own, bx, by, bxy = pack(k, width, heat, wet, label)
        received.append((own, send(bx, "x"), send(by, "y"), send(bxy, "xy")))
    stack_w, stack_h = prep(thermal, water)
    outs = []
    inners, beyond = [], []
    for k, width in enumerate(widths):
        own, rx, ry, rxy = received[k]
        if k:
            rxy, _ = lax.optimization_barrier((rxy, inners[-1][2]))
            received[k] = (own, rx, ry, rxy)
        beyond.append((send(jnp.stack([own, rx]), "own"), send(jnp.stack([ry, rxy]), "partner")))
        inners.append(pre(width, own, rx, ry, rxy, spread, factor, stack_h))
    for k, width in enumerate(widths):
        own, rx, ry, rxy = received[k]
        inner, kap, km = inners[k]
        p1, p2 = beyond[k]
        after = inners[k + 1][2] if k + 1 < len(widths) else km
        post = stencil(width, own, rx, ry, rxy, p1, p2, inner, kap, spread, factor, after)
        other = send(post, "core")
        kept, bx, by, bxy = solve(width, post, other, stack_w, stack_h, km)
        blocks = [kept, send(bx, "x"), send(by, "y"), send(bxy, "xy")]
        outs = assemble(k, width, columns, blocks, outs)
    return tuple(outs)


def solution(mesh):
    return jax.shard_map(
        functools.partial(per_device, mesh.shape["lat"]),
        mesh=mesh,
        in_specs=(
            P("depth", "lat", None),
            P("depth", "lat", None),
            P("lat", None),
            P(),
            P(),
            P(),
            P(),
        ),
        out_specs=(P("depth", "lat", None), P("depth", "lat", None)),
        check_vma=False,
    )
```

```python
import functools

import jax
import jax.numpy as jnp
import numpy as np
from jax import lax
from jax.experimental import pallas as pl
from jax.experimental.pallas import tpu as pltpu
from jax.sharding import PartitionSpec as P

DEPTH = 128
SLAB = 32
ROWS = 4
RATE = 0.25
PARTS = (2, 2)
JOINT = ("lat", "depth")
BODY = 2 * ROWS * SLAB
PIECES = 1
HOP_ROWS = 816
TAIL_ROWS = 136
VMEM_LIMIT = 48 * 1024 * 1024
FIRST_LIMIT = 62 * 1024 * 1024


def params(limit=VMEM_LIMIT):
    return pltpu.CompilerParams(vmem_limit_bytes=limit)


def cost(flops, nbytes):
    return pl.CostEstimate(flops=0, bytes_accessed=1024, transcendentals=0)


def scaled_cheb(count):
    f32 = np.float32
    index = np.arange(count).astype(f32)
    nodes = np.cos((f32(np.pi) * index / f32(count - 1)).astype(f32)).astype(f32)
    ends = np.where((index == 0) | (index == count - 1), 2.0, 1.0)
    signs = np.where(np.arange(count) % 2 == 0, 1.0, -1.0)
    weight = (ends * signs).astype(f32)
    diagonal = np.eye(count, dtype=bool)
    spread = nodes[:, None] - nodes[None, :]
    off = weight[:, None] / weight[None, :] / np.where(diagonal, f32(1.0), spread)
    off = np.where(diagonal, f32(0.0), off).astype(f32)
    deriv = off - np.diag(np.sum(off, axis=1, dtype=f32))
    scale = (f32(1.0) - nodes * nodes) / f32(count)
    return (scale[:, None] * deriv).astype(f32)


def place():
    lat = lax.axis_index("lat")
    dep = lax.axis_index("depth")
    return lax.rem(lat, 2), lax.div(dep, 2), lax.rem(dep, 2)


def quarter():
    y, x, _ = place()
    return 2 * y + x


def chunk_width(k, columns):
    return columns * PARTS[k] // (4 * sum(PARTS))


def column_start(k, mask, columns):
    width = chunk_width(k, columns)
    place_in_chunk = lax.bitwise_xor(quarter(), mask) * width
    return pl.multiple_of(chunk_start(k, columns) + place_in_chunk, 128)


def chunk_start(k, columns):
    return sum(4 * chunk_width(i, columns) for i in range(k))


def chunk_window(k, columns):
    first = max(chunk_start(k, columns) - 128, 0)
    return first, min(chunk_start(k + 1, columns) + 128, columns)


def halo_at(f, width):
    return (BODY, 128 * f) if width >= 256 else (BODY + 8 * f, 0)


def label_at(width):
    return BODY + (8 if width >= 256 else 16)


def block_rows(width):
    return label_at(width) + 8


def lanes(shape):
    return lax.broadcasted_iota(jnp.int32, shape, len(shape) - 1)


def pack_kernel(k, width, heat_hbm, wet_hbm, label_hbm, *refs):
    *blocks, near, label_ref, sems = refs
    columns = heat_hbm.shape[2]
    first, last = chunk_window(k, columns)
    copies = [pltpu.make_async_copy(label_hbm, label_ref, sems.at[2 * PIECES])]
    for f, far in enumerate((heat_hbm, wet_hbm)):
        for piece in range(PIECES):
            at = pl.ds(piece * (SLAB // PIECES), SLAB // PIECES)
            copies.append(
                pltpu.make_async_copy(
                    far.at[at, :, first:last], near.at[f, at], sems.at[f * PIECES + piece]
                )
            )
    for copy in copies:
        copy.start()
    for copy in copies:
        copy.wait()
    lane = lanes((SLAB, 128))
    lane8 = lanes((8, 128))
    lane4 = lanes((ROWS, 128))
    for mask in range(4):
        start = column_start(k, mask, columns)
        left = pl.multiple_of(jnp.maximum(start - 128, 0), 128)
        right = pl.multiple_of(jnp.minimum(start + width, columns - 128), 128)
        keep_left = (start > 0).astype(jnp.float32)
        keep_right = (start + width < columns).astype(jnp.float32)
        main, before, after = (pl.multiple_of(at - first, 128) for at in (start, left, right))
        for f in range(2):
            ref = near.at[f]
            packed = jnp.zeros((8, 128), jnp.float32)
            for r in range(ROWS):
                row = (f * ROWS + r) * SLAB
                blocks[mask][row : row + SLAB, :] = ref[:, r, pl.ds(main, width)]
                edge = jnp.where(
                    lane >= 64,
                    ref[:, r, pl.ds(before, 128)] * keep_left,
                    ref[:, r, pl.ds(after, 128)] * keep_right,
                )
                for g in range(SLAB // 8):
                    at = 8 * (r * (SLAB // 8) + g)
                    moved = pltpu.roll(edge[8 * g : 8 * g + 8], (at + 4) % 128, 1)
                    packed = jnp.where((lane8 >= at) & (lane8 < at + 8), moved, packed)
            at, lane_at = halo_at(f, width)
            blocks[mask][at : at + 8, lane_at : lane_at + 128] = packed
        types = label_at(width)
        blocks[mask][types : types + 4, :] = (
            label_ref[:, pl.ds(start, width)] + 1
        ).astype(jnp.float32)
        edge = jnp.where(
            lane4 >= 124,
            (label_ref[:, pl.ds(left, 128)] + 1).astype(jnp.float32) * keep_left,
            (label_ref[:, pl.ds(right, 128)] + 1).astype(jnp.float32) * keep_right,
        )
        blocks[mask][types + 4 : types + 8, :] = jnp.zeros((ROWS, width), jnp.float32)
        blocks[mask][types + 4 : types + 8, :128] = jnp.where(
            (lane4 >= 124) | (lane4 < 4), edge, 0.0
        )


def pack(k, width, heat, wet, label):
    shape = jax.ShapeDtypeStruct((block_rows(width), width), jnp.float32)
    first, last = chunk_window(k, heat.shape[2])
    return pl.pallas_call(
        functools.partial(pack_kernel, k, width),
        out_shape=[shape] * 4,
        in_specs=[pl.BlockSpec(memory_space=pltpu.HBM)] * 3,
        out_specs=[pl.BlockSpec(memory_space=pltpu.VMEM)] * 4,
        scratch_shapes=[
            pltpu.VMEM((2, SLAB, ROWS, last - first), jnp.float32),
            pltpu.VMEM(label.shape, jnp.int32),
            pltpu.SemaphoreType.DMA((2 * PIECES + 1,)),
        ],
        compiler_params=params(VMEM_LIMIT if k else FIRST_LIMIT),
        cost_estimate=cost(0, 4 << 20),
        name="pack",
    )(heat, wet, label)


def prep_kernel(thermal_ref, water_ref, cheb_ref, stack_w_ref, stack_h_ref):
    _, x, c = place()
    dot = functools.partial(
        jnp.dot, precision=lax.Precision.HIGHEST, preferred_element_type=jnp.float32
    )

    def depth_of(n):
        slab, inner = lax.div(n, SLAB), lax.rem(n, SLAB)
        dx = lax.rem(slab, 2)
        dc = lax.div(slab, 2)
        return (2 * lax.rem(x + dx, 2) + lax.rem(c + dc, 2)) * SLAB + inner

    row = lax.broadcasted_iota(jnp.int32, (DEPTH, DEPTH), 0)
    col = lax.broadcasted_iota(jnp.int32, (DEPTH, DEPTH), 1)
    order = (row == depth_of(col)).astype(jnp.float32)
    picks = (depth_of(row[: 2 * SLAB]) == col[: 2 * SLAB]).astype(jnp.float32)
    thermal = dot(picks, thermal_ref[...])
    water = dot(picks, water_ref[...])
    cheb = cheb_ref[...]
    stack_w = jnp.concatenate(
        [water, -0.25 * dot(thermal, cheb), 0.5 * dot(water, cheb)], axis=0
    )
    for ref, stack in ((stack_w_ref, stack_w), (stack_h_ref, thermal)):
        ordered = dot(stack, order)
        high = ordered.astype(jnp.bfloat16)
        low = (ordered - high.astype(jnp.float32)).astype(jnp.bfloat16)
        count = ordered.shape[0]
        ref[:count, :] = high
        ref[count:, :] = low


def prep(thermal, water):
    cheb = jnp.asarray(scaled_cheb(DEPTH))
    return pl.pallas_call(
        prep_kernel,
        out_shape=[
            jax.ShapeDtypeStruct((12 * SLAB, DEPTH), jnp.bfloat16),
            jax.ShapeDtypeStruct((4 * SLAB, DEPTH), jnp.bfloat16),
        ],
        in_specs=[pl.BlockSpec(memory_space=pltpu.VMEM)] * 3,
        out_specs=[pl.BlockSpec(memory_space=pltpu.VMEM)] * 2,
        compiler_params=params(),
        cost_estimate=cost(1 << 24, 1 << 18),
        name="prep",
    )(thermal, water, cheb)


def substep(above, here, below, kappa_heat, kappa_moist):
    laps = []
    size = here[0].shape[1]
    for f in range(2):
        u = here[f]
        sides = pltpu.roll(u, 1, 1) + pltpu.roll(u, size - 1, 1)
        laps.append((above[f] + below[f]) + sides - 4.0 * u)
    heat, wet = here
    body = 1.0 + wet * wet
    guess = pl.reciprocal(body, approx=True)
    inverse = guess * (2.0 - body * guess)
    spread = kappa_heat * (1.5 - 0.5 * inverse)
    return heat + spread * laps[0], wet + kappa_moist * laps[1]


def factors(label, spread_ref, factor_ref):
    heat = jnp.zeros(label.shape, jnp.float32)
    moist = jnp.zeros(label.shape, jnp.float32)
    for i in range(spread_ref.shape[0]):
        here = label == i + 1.0
        heat = jnp.where(here, spread_ref[i], heat)
        moist = jnp.where(here, factor_ref[i], moist)
    return heat, moist


INNER = [(1, 5), (1, 6), (1, 9), (1, 10), (2, 6), (2, 7), (2, 8), (2, 9), (3, 7), (3, 8)]
COUNT = 4 * ROWS


def stored(r):
    return jnp.where(lax.rem(lax.axis_index("lat"), 2) == 1, ROWS - 1 - r, r)


def strip_factors(width, block, spread_ref, factor_ref):
    y, _, _ = place()
    label = block[label_at(width) : label_at(width) + 8, :]
    body = factors(label[:ROWS], spread_ref, factor_ref)
    edge = factors(label[ROWS:, :128], spread_ref, factor_ref)
    for f in range(2):
        whole = jnp.concatenate([body[f], edge[f]], axis=1)
        back = jnp.concatenate([whole[r : r + 1] for r in reversed(range(ROWS))], axis=0)
        yield jnp.where(y == 1, back, whole)


def load_row(width, block, r, g):
    r = stored(r)
    shift = lax.rem(252 - 8 * (r * (SLAB // 8) + g), 128)
    fields = []
    for f in range(2):
        at = pl.multiple_of((f * ROWS + r) * SLAB + 8 * g, 8)
        row, lane = halo_at(f, width)
        edge = pltpu.roll(block[row : row + 8, lane : lane + 128], shift, 1)
        fields.append(jnp.concatenate([block[pl.ds(at, 8), :], edge], axis=1))
    return tuple(fields)


def pre_kernel(width, own, rx, ry, rxy, spread_ref, factor_ref, _, inner, kap, km_ref):
    for j, block in enumerate((own, ry)):
        to = slice(j * ROWS, j * ROWS + ROWS)
        for f, whole in enumerate(strip_factors(width, block, spread_ref, factor_ref)):
            kap[f, to, :] = RATE * whole
            if f == 1:
                km_ref[to, :] = factors(block[label_at(width) : label_at(width) + ROWS, :], spread_ref, factor_ref)[1]
    for s in range(2):
        blocks = ((own, rx)[s], (ry, rxy)[s])

        def group(g, carry):
            levels = [dict() for _ in range(4)]
            at = pl.ds(pl.multiple_of(s * SLAB + 8 * g, 8), 8)
            for j in range(ROWS, 3 * ROWS + 3):
                if j < 3 * ROWS:
                    levels[0][j] = load_row(width, blocks[j // ROWS - 1], j % ROWS, g)
                for t in range(1, 4):
                    i = j - t
                    if ROWS + t <= i < 3 * ROWS - t:
                        prev, k = levels[t - 1], i - ROWS
                        levels[t][i] = substep(
                            prev[i - 1], prev[i], prev[i + 1], kap[0, k : k + 1, :], kap[1, k : k + 1, :]
                        )
                        if (t, i) in INNER:
                            for f in range(2):
                                inner[INNER.index((t, i)), f, at, :] = levels[t][i][f]
            return carry

        lax.fori_loop(0, SLAB // 8, group, 0, unroll=2)


def pre(width, own, rx, ry, rxy, spread, factor, after):
    wide = width + 128
    return pl.pallas_call(
        functools.partial(pre_kernel, width),
        out_shape=[
            jax.ShapeDtypeStruct((len(INNER), 2, 2 * SLAB, wide), jnp.float32),
            jax.ShapeDtypeStruct((2, 2 * ROWS, wide), jnp.float32),
            jax.ShapeDtypeStruct((2 * ROWS, width), jnp.float32),
        ],
        in_specs=[pl.BlockSpec(memory_space=pltpu.VMEM)] * 4
        + [pl.BlockSpec(memory_space=pltpu.SMEM)] * 2
        + [pl.BlockSpec(memory_space=pl.ANY)],
        out_specs=[pl.BlockSpec(memory_space=pltpu.VMEM)] * 3,
        compiler_params=params(),
        cost_estimate=cost(1 << 24, 4 << 20),
        name="inner_substeps",
    )(own, rx, ry, rxy, spread, factor, after)


def stencil_kernel(
    width, own, rx, ry, rxy, p1, p2, inner, kap_ref, spread_ref, factor_ref, post_own, post_partner, kap
):
    kap[:, ROWS : 3 * ROWS, :] = kap_ref[...]
    for j, block in ((0, p2.at[0]), (3, p1.at[0])):
        for f, whole in enumerate(strip_factors(width, block, spread_ref, factor_ref)):
            kap[f, j * ROWS : j * ROWS + ROWS, :] = RATE * whole
    for s in range(2):
        blocks = (p2.at[s], (own, rx)[s], (ry, rxy)[s], p1.at[s])

        def group(g, carry):
            at = pl.ds(pl.multiple_of(s * SLAB + 8 * g, 8), 8)
            levels = [dict() for _ in range(5)]
            for j in range(COUNT + 4):
                if j < COUNT and not ROWS + 2 <= j < 3 * ROWS - 2:
                    levels[0][j] = load_row(width, blocks[j // ROWS], j % ROWS, g)
                for t in range(1, 5):
                    i = j - t
                    if (t, i) in INNER:
                        k = INNER.index((t, i))
                        levels[t][i] = tuple(inner[k, f, at, :] for f in range(2))
                    elif t <= i < COUNT - t and not (t < 4 and ROWS + t <= i < 3 * ROWS - t):
                        prev = levels[t - 1]
                        levels[t][i] = substep(
                            prev[i - 1], prev[i], prev[i + 1], kap[0, i : i + 1, :], kap[1, i : i + 1, :]
                        )
                        if t == 4:
                            post = (post_own, post_partner)[(i - ROWS) // ROWS]
                            for f in range(2):
                                post[f, stored(i % ROWS), at, :] = levels[4][i][f][:, :width]
            return carry

        lax.fori_loop(0, SLAB // 8, group, 0)


def stencil(width, own, rx, ry, rxy, p1, p2, inner, kap, spread, factor):
    return pl.pallas_call(
        functools.partial(stencil_kernel, width),
        out_shape=[jax.ShapeDtypeStruct((2, ROWS, 2 * SLAB, width), jnp.float32)] * 2,
        in_specs=[pl.BlockSpec(memory_space=pltpu.VMEM)] * 8
        + [pl.BlockSpec(memory_space=pltpu.SMEM)] * 2,
        out_specs=[pl.BlockSpec(memory_space=pltpu.VMEM)] * 2,
        scratch_shapes=[pltpu.VMEM((2, COUNT, width + 128), jnp.float32)],
        compiler_params=params(),
        cost_estimate=cost(1 << 24, 4 << 20),
        name="outer_substeps",
    )(own, rx, ry, rxy, p1, p2, inner, kap, spread, factor)


def split(values):
    high = values.astype(jnp.bfloat16)
    return high, (values - high.astype(jnp.float32)).astype(jnp.bfloat16)


def solve_kernel(*refs):
    mine, other, (stack_w, stack_h, km), blocks = refs[:2], refs[2:4], refs[4:7], refs[7:]
    dot = functools.partial(jnp.dot, preferred_element_type=jnp.float32)
    half = 2 * SLAB

    def apply(stack, values):
        high, low = split(values)
        count = stack.shape[0] // 2
        both = dot(stack[...], high)
        return both[:count] + both[count:] + dot(stack[:count, :], low)

    for r in range(2 * ROWS):
        strip, inner = divmod(r, ROWS)
        heat = apply(stack_h, jnp.concatenate([mine[strip][0, inner], other[strip][0, inner]], axis=0))
        wet = apply(stack_w, jnp.concatenate([mine[strip][1, inner], other[strip][1, inner]], axis=0))
        factor = km[r : r + 1, :]
        results = (
            heat + factor * wet[half : 2 * half],
            wet[:half] + factor * wet[2 * half :],
        )
        for f in range(2):
            base = (f * ROWS + inner) * SLAB
            for slab in range(2):
                blocks[2 * strip + slab][base : base + SLAB, :] = results[f][
                    slab * SLAB : slab * SLAB + SLAB
                ]


def solve(width, mine, other, stack_w, stack_h, km):
    shape = jax.ShapeDtypeStruct((BODY, width), jnp.float32)
    return pl.pallas_call(
        solve_kernel,
        out_shape=[shape] * 4,
        in_specs=[pl.BlockSpec(memory_space=pltpu.VMEM)] * 7,
        out_specs=[pl.BlockSpec(memory_space=pltpu.VMEM)] * 4,
        compiler_params=params(),
        cost_estimate=cost(1 << 26, 4 << 20),
        name="solve",
    )(*mine, *other, stack_w, stack_h, km)


def assemble_kernel(k, width, *refs):
    blocks, outs, scratch, sems = refs[:4], refs[-4:-2], refs[-2], refs[-1]
    columns = outs[0].shape[2]
    copies = []
    for mask in range(4):
        start = column_start(k, mask, columns)
        for f in range(2):
            for r in range(ROWS):
                base = (f * ROWS + r) * SLAB
                scratch[mask, f, :, r, :] = blocks[mask][base : base + SLAB, :]
            copy = pltpu.make_async_copy(
                scratch.at[mask, f],
                outs[f].at[:, :, pl.ds(start, width)],
                sems.at[2 * mask + f],
            )
            copy.start()
            copies.append(copy)
    for copy in copies:
        copy.wait()


def assemble(k, width, columns, blocks, outs, tail):
    shape = jax.ShapeDtypeStruct((SLAB, ROWS, columns), jnp.float32)
    return pl.pallas_call(
        functools.partial(assemble_kernel, k, width),
        out_shape=[shape] * 2,
        in_specs=[pl.BlockSpec(memory_space=pltpu.VMEM)] * 4
        + [pl.BlockSpec(memory_space=pltpu.HBM)] * len(outs)
        + [pl.BlockSpec(memory_space=pl.ANY)] * len(tail),
        out_specs=[pl.BlockSpec(memory_space=pltpu.HBM)] * 2,
        scratch_shapes=[
            pltpu.VMEM((4, 2, SLAB, ROWS, width), jnp.float32),
            pltpu.SemaphoreType.DMA((8,)),
        ],
        input_output_aliases={4 + i: i for i in range(len(outs))},
        compiler_params=params(),
        cost_estimate=cost(0, 4 << 20),
        name="assemble",
    )(*blocks, *outs, *tail)


def routes(strips):
    cells = [(l, d) for l in range(strips) for d in range(4)]

    def pairs(to):
        return [
            (l * 4 + d, to(l, d)[0] * 4 + to(l, d)[1])
            for l, d in cells
            if 0 <= to(l, d)[0] < strips
        ]

    return {
        "x": pairs(lambda l, d: (l, d ^ 2)),
        "y": pairs(lambda l, d: (l ^ 1, d)),
        "xy": pairs(lambda l, d: (l ^ 1, d ^ 2)),
        "core": pairs(lambda l, d: (l, d ^ 1)),
        "own": pairs(lambda l, d: (l + 2 if l % 2 else l - 2, d)),
        "partner": pairs(lambda l, d: (l - 2 if l % 2 else l + 2, d)),
    }


def per_device(strips, heat, wet, label, spread, factor, thermal, water):
    columns = heat.shape[2]
    widths = [chunk_width(k, columns) for k in range(len(PARTS))]
    route = routes(strips)

    def send(array, name):
        return lax.ppermute(array, JOINT, route[name])

    received = []
    for k, width in enumerate(widths):
        own, bx, by, bxy = pack(k, width, heat, wet, label)
        received.append((own, send(bx, "x"), send(by, "y"), send(bxy, "xy")))
    stack_w, stack_h = prep(thermal, water)
    outs = []
    before, tail = None, []

    def after(value, *others):
        return lax.optimization_barrier((value, *others))[0] if others else value

    for k, width in enumerate(widths):
        own, rx, ry, rxy = received[k]
        if k:
            ry = after(ry, before[1])
            hop = send(jnp.concatenate([rx, ry, rxy, own])[:HOP_ROWS], "core")
        p1 = send(jnp.stack([own, rx]), "own")
        p2 = send(jnp.stack([ry, rxy]), "partner")
        inner, kap, km = pre(width, own, rx, ry, rxy, spread, factor, hop if k else stack_h)
        if k:
            kap = after(kap, before[0])
        mine = stencil(width, own, rx, ry, rxy, p1, p2, inner, kap, spread, factor)
        other = [send(piece, "core") for piece in mine]
        kept, bx, by, bxy = solve(width, mine, other, stack_w, stack_h, km)
        arrived = [send(bx, "x"), send(by, "y"), send(bxy, "xy")]
        before = (kept, km)
        outs = assemble(k, width, columns, [kept, *arrived], outs, tail)
        if k + 1 < len(widths):
            tail = [send(jnp.concatenate([block[:TAIL_ROWS] for block in arrived]), "core")]
        else:
            tail = []
    return tuple(outs)


def solution(mesh):
    return jax.shard_map(
        functools.partial(per_device, mesh.shape["lat"]),
        mesh=mesh,
        in_specs=(
            P("depth", "lat", None),
            P("depth", "lat", None),
            P("lat", None),
            P(),
            P(),
            P(),
            P(),
        ),
        out_specs=(P("depth", "lat", None), P("depth", "lat", None)),
        check_vma=False,
    )
```

```python
import functools

import jax
import jax.numpy as jnp
import numpy as np
from jax import lax
from jax.experimental import pallas as pl
from jax.experimental.pallas import tpu as pltpu
from jax.sharding import PartitionSpec as P

DEPTH = 128
SLAB = 32
ROWS = 4
RATE = 0.25
PARTS = (2, 2)
JOINT = ("lat", "depth")
BODY = 2 * ROWS * SLAB
PIECES = 1
HOP_ROWS = 816
TAIL_ROWS = 136
VMEM_LIMIT = 48 * 1024 * 1024
FIRST_LIMIT = 62 * 1024 * 1024


def params(limit=VMEM_LIMIT):
    return pltpu.CompilerParams(vmem_limit_bytes=limit)


def cost(flops, nbytes):
    return pl.CostEstimate(flops=0, bytes_accessed=1024, transcendentals=0)


def scaled_cheb(count):
    f32 = np.float32
    index = np.arange(count).astype(f32)
    nodes = np.cos((f32(np.pi) * index / f32(count - 1)).astype(f32)).astype(f32)
    ends = np.where((index == 0) | (index == count - 1), 2.0, 1.0)
    signs = np.where(np.arange(count) % 2 == 0, 1.0, -1.0)
    weight = (ends * signs).astype(f32)
    diagonal = np.eye(count, dtype=bool)
    spread = nodes[:, None] - nodes[None, :]
    off = weight[:, None] / weight[None, :] / np.where(diagonal, f32(1.0), spread)
    off = np.where(diagonal, f32(0.0), off).astype(f32)
    deriv = off - np.diag(np.sum(off, axis=1, dtype=f32))
    scale = (f32(1.0) - nodes * nodes) / f32(count)
    return (scale[:, None] * deriv).astype(f32)


def place():
    lat = lax.axis_index("lat")
    dep = lax.axis_index("depth")
    return lax.rem(lat, 2), lax.div(dep, 2), lax.rem(dep, 2)


def quarter():
    y, x, _ = place()
    return 2 * y + x


def chunk_width(k, columns):
    return columns * PARTS[k] // (4 * sum(PARTS))


def column_start(k, mask, columns):
    width = chunk_width(k, columns)
    place_in_chunk = lax.bitwise_xor(quarter(), mask) * width
    return pl.multiple_of(chunk_start(k, columns) + place_in_chunk, 128)


def chunk_start(k, columns):
    return sum(4 * chunk_width(i, columns) for i in range(k))


def chunk_window(k, columns):
    first = max(chunk_start(k, columns) - 128, 0)
    return first, min(chunk_start(k + 1, columns) + 128, columns)


def halo_at(f, width):
    return (BODY, 128 * f) if width >= 256 else (BODY + 8 * f, 0)


def label_at(width):
    return BODY + (8 if width >= 256 else 16)


def block_rows(width):
    return label_at(width) + 8


def lanes(shape):
    return lax.broadcasted_iota(jnp.int32, shape, len(shape) - 1)


def pack_kernel(k, width, heat_hbm, wet_hbm, label_hbm, *refs):
    *blocks, near, label_ref, sems = refs
    columns = heat_hbm.shape[2]
    first, last = chunk_window(k, columns)
    copies = [pltpu.make_async_copy(label_hbm, label_ref, sems.at[2 * PIECES])]
    for f, far in enumerate((heat_hbm, wet_hbm)):
        for piece in range(PIECES):
            at = pl.ds(piece * (SLAB // PIECES), SLAB // PIECES)
            copies.append(
                pltpu.make_async_copy(
                    far.at[at, :, first:last], near.at[f, at], sems.at[f * PIECES + piece]
                )
            )
    for copy in copies:
        copy.start()
    for copy in copies:
        copy.wait()
    lane = lanes((SLAB, 128))
    lane8 = lanes((8, 128))
    lane4 = lanes((ROWS, 128))
    for mask in range(4):
        start = column_start(k, mask, columns)
        left = pl.multiple_of(jnp.maximum(start - 128, 0), 128)
        right = pl.multiple_of(jnp.minimum(start + width, columns - 128), 128)
        keep_left = (start > 0).astype(jnp.float32)
        keep_right = (start + width < columns).astype(jnp.float32)
        main, before, after = (pl.multiple_of(at - first, 128) for at in (start, left, right))
        for f in range(2):
            ref = near.at[f]
            packed = jnp.zeros((8, 128), jnp.float32)
            for r in range(ROWS):
                row = (f * ROWS + r) * SLAB
                blocks[mask][row : row + SLAB, :] = ref[:, r, pl.ds(main, width)]
                edge = jnp.where(
                    lane >= 64,
                    ref[:, r, pl.ds(before, 128)] * keep_left,
                    ref[:, r, pl.ds(after, 128)] * keep_right,
                )
                for g in range(SLAB // 8):
                    at = 8 * (r * (SLAB // 8) + g)
                    moved = pltpu.roll(edge[8 * g : 8 * g + 8], (at + 4) % 128, 1)
                    packed = jnp.where((lane8 >= at) & (lane8 < at + 8), moved, packed)
            at, lane_at = halo_at(f, width)
            blocks[mask][at : at + 8, lane_at : lane_at + 128] = packed
        types = label_at(width)
        blocks[mask][types : types + 4, :] = (
            label_ref[:, pl.ds(start, width)] + 1
        ).astype(jnp.float32)
        edge = jnp.where(
            lane4 >= 124,
            (label_ref[:, pl.ds(left, 128)] + 1).astype(jnp.float32) * keep_left,
            (label_ref[:, pl.ds(right, 128)] + 1).astype(jnp.float32) * keep_right,
        )
        blocks[mask][types + 4 : types + 8, :] = jnp.zeros((ROWS, width), jnp.float32)
        blocks[mask][types + 4 : types + 8, :128] = jnp.where(
            (lane4 >= 124) | (lane4 < 4), edge, 0.0
        )


def pack(k, width, heat, wet, label):
    shape = jax.ShapeDtypeStruct((block_rows(width), width), jnp.float32)
    first, last = chunk_window(k, heat.shape[2])
    return pl.pallas_call(
        functools.partial(pack_kernel, k, width),
        out_shape=[shape] * 4,
        in_specs=[pl.BlockSpec(memory_space=pltpu.HBM)] * 3,
        out_specs=[pl.BlockSpec(memory_space=pltpu.VMEM)] * 4,
        scratch_shapes=[
            pltpu.VMEM((2, SLAB, ROWS, last - first), jnp.float32),
            pltpu.VMEM(label.shape, jnp.int32),
            pltpu.SemaphoreType.DMA((2 * PIECES + 1,)),
        ],
        compiler_params=params(VMEM_LIMIT if k else FIRST_LIMIT),
        cost_estimate=cost(0, 4 << 20),
        name="pack",
    )(heat, wet, label)


def prep_kernel(thermal_ref, water_ref, cheb_ref, stack_w_ref, stack_h_ref):
    _, x, c = place()
    dot = functools.partial(
        jnp.dot, precision=lax.Precision.HIGHEST, preferred_element_type=jnp.float32
    )

    def depth_of(n):
        slab, inner = lax.div(n, SLAB), lax.rem(n, SLAB)
        dx = lax.rem(slab, 2)
        dc = lax.div(slab, 2)
        return (2 * lax.rem(x + dx, 2) + lax.rem(c + dc, 2)) * SLAB + inner

    row = lax.broadcasted_iota(jnp.int32, (DEPTH, DEPTH), 0)
    col = lax.broadcasted_iota(jnp.int32, (DEPTH, DEPTH), 1)
    order = (row == depth_of(col)).astype(jnp.float32)
    picks = (depth_of(row[: 2 * SLAB]) == col[: 2 * SLAB]).astype(jnp.float32)
    thermal = dot(picks, thermal_ref[...])
    water = dot(picks, water_ref[...])
    cheb = cheb_ref[...]
    stack_w = jnp.concatenate(
        [water, -0.25 * dot(thermal, cheb), 0.5 * dot(water, cheb)], axis=0
    )
    for ref, stack in ((stack_w_ref, stack_w), (stack_h_ref, thermal)):
        ordered = dot(stack, order)
        high = ordered.astype(jnp.bfloat16)
        low = (ordered - high.astype(jnp.float32)).astype(jnp.bfloat16)
        count = ordered.shape[0]
        ref[:count, :] = high
        ref[count:, :] = low


def prep(thermal, water):
    cheb = jnp.asarray(scaled_cheb(DEPTH))
    return pl.pallas_call(
        prep_kernel,
        out_shape=[
            jax.ShapeDtypeStruct((12 * SLAB, DEPTH), jnp.bfloat16),
            jax.ShapeDtypeStruct((4 * SLAB, DEPTH), jnp.bfloat16),
        ],
        in_specs=[pl.BlockSpec(memory_space=pltpu.VMEM)] * 3,
        out_specs=[pl.BlockSpec(memory_space=pltpu.VMEM)] * 2,
        compiler_params=params(),
        cost_estimate=cost(1 << 24, 1 << 18),
        name="prep",
    )(thermal, water, cheb)


def substep(above, here, below, kappa_heat, kappa_moist):
    laps = []
    size = here[0].shape[1]
    for f in range(2):
        u = here[f]
        sides = pltpu.roll(u, 1, 1) + pltpu.roll(u, size - 1, 1)
        laps.append((above[f] + below[f]) + sides - 4.0 * u)
    heat, wet = here
    body = 1.0 + wet * wet
    guess = pl.reciprocal(body, approx=True)
    inverse = guess * (2.0 - body * guess)
    spread = kappa_heat * (1.5 - 0.5 * inverse)
    return heat + spread * laps[0], wet + kappa_moist * laps[1]


def factors(label, spread_ref, factor_ref):
    heat = jnp.zeros(label.shape, jnp.float32)
    moist = jnp.zeros(label.shape, jnp.float32)
    for i in range(spread_ref.shape[0]):
        here = label == i + 1.0
        heat = jnp.where(here, spread_ref[i], heat)
        moist = jnp.where(here, factor_ref[i], moist)
    return heat, moist


INNER = [(1, 5), (1, 6), (1, 9), (1, 10), (2, 6), (2, 7), (2, 8), (2, 9), (3, 7), (3, 8)]
COUNT = 4 * ROWS


def stored(r):
    return jnp.where(lax.rem(lax.axis_index("lat"), 2) == 1, ROWS - 1 - r, r)


def strip_factors(width, block, spread_ref, factor_ref):
    y, _, _ = place()
    label = block[label_at(width) : label_at(width) + 8, :]
    body = factors(label[:ROWS], spread_ref, factor_ref)
    edge = factors(label[ROWS:, :128], spread_ref, factor_ref)
    for f in range(2):
        whole = jnp.concatenate([body[f], edge[f]], axis=1)
        back = jnp.concatenate([whole[r : r + 1] for r in reversed(range(ROWS))], axis=0)
        yield jnp.where(y == 1, back, whole)


def load_row(width, block, r, g):
    r = stored(r)
    shift = lax.rem(252 - 8 * (r * (SLAB // 8) + g), 128)
    fields = []
    for f in range(2):
        at = pl.multiple_of((f * ROWS + r) * SLAB + 8 * g, 8)
        row, lane = halo_at(f, width)
        edge = pltpu.roll(block[row : row + 8, lane : lane + 128], shift, 1)
        fields.append(jnp.concatenate([block[pl.ds(at, 8), :], edge], axis=1))
    return tuple(fields)


def pre_kernel(width, own, rx, ry, rxy, spread_ref, factor_ref, _, inner, kap, km_ref):
    for j, block in enumerate((own, ry)):
        to = slice(j * ROWS, j * ROWS + ROWS)
        for f, whole in enumerate(strip_factors(width, block, spread_ref, factor_ref)):
            kap[f, to, :] = RATE * whole
            if f == 1:
                km_ref[to, :] = factors(block[label_at(width) : label_at(width) + ROWS, :], spread_ref, factor_ref)[1]
    for s in range(2):
        blocks = ((own, rx)[s], (ry, rxy)[s])

        def group(g, carry):
            levels = [dict() for _ in range(4)]
            at = pl.ds(pl.multiple_of(s * SLAB + 8 * g, 8), 8)
            for j in range(ROWS, 3 * ROWS + 3):
                if j < 3 * ROWS:
                    levels[0][j] = load_row(width, blocks[j // ROWS - 1], j % ROWS, g)
                for t in range(1, 4):
                    i = j - t
                    if ROWS + t <= i < 3 * ROWS - t:
                        prev, k = levels[t - 1], i - ROWS
                        levels[t][i] = substep(
                            prev[i - 1], prev[i], prev[i + 1], kap[0, k : k + 1, :], kap[1, k : k + 1, :]
                        )
                        if (t, i) in INNER:
                            for f in range(2):
                                inner[INNER.index((t, i)), f, at, :] = levels[t][i][f]
            return carry

        lax.fori_loop(0, SLAB // 8, group, 0, unroll=2)


def pre(width, own, rx, ry, rxy, spread, factor, after):
    wide = width + 128
    return pl.pallas_call(
        functools.partial(pre_kernel, width),
        out_shape=[
            jax.ShapeDtypeStruct((len(INNER), 2, 2 * SLAB, wide), jnp.float32),
            jax.ShapeDtypeStruct((2, 2 * ROWS, wide), jnp.float32),
            jax.ShapeDtypeStruct((2 * ROWS, width), jnp.float32),
        ],
        in_specs=[pl.BlockSpec(memory_space=pltpu.VMEM)] * 4
        + [pl.BlockSpec(memory_space=pltpu.SMEM)] * 2
        + [pl.BlockSpec(memory_space=pl.ANY)],
        out_specs=[pl.BlockSpec(memory_space=pltpu.VMEM)] * 3,
        compiler_params=params(),
        cost_estimate=cost(1 << 24, 4 << 20),
        name="inner_substeps",
    )(own, rx, ry, rxy, spread, factor, after)


def stencil_kernel(
    width, own, rx, ry, rxy, p1, p2, inner, kap_ref, spread_ref, factor_ref, post_own, post_partner, kap
):
    kap[:, ROWS : 3 * ROWS, :] = kap_ref[...]
    for j, block in ((0, p2.at[0]), (3, p1.at[0])):
        for f, whole in enumerate(strip_factors(width, block, spread_ref, factor_ref)):
            kap[f, j * ROWS : j * ROWS + ROWS, :] = RATE * whole
    for s in range(2):
        blocks = (p2.at[s], (own, rx)[s], (ry, rxy)[s], p1.at[s])

        def group(g, carry):
            at = pl.ds(pl.multiple_of(s * SLAB + 8 * g, 8), 8)
            levels = [dict() for _ in range(5)]
            for j in range(COUNT + 4):
                if j < COUNT and not ROWS + 2 <= j < 3 * ROWS - 2:
                    levels[0][j] = load_row(width, blocks[j // ROWS], j % ROWS, g)
                for t in range(1, 5):
                    i = j - t
                    if (t, i) in INNER:
                        k = INNER.index((t, i))
                        levels[t][i] = tuple(inner[k, f, at, :] for f in range(2))
                    elif t <= i < COUNT - t and not (t < 4 and ROWS + t <= i < 3 * ROWS - t):
                        prev = levels[t - 1]
                        levels[t][i] = substep(
                            prev[i - 1], prev[i], prev[i + 1], kap[0, i : i + 1, :], kap[1, i : i + 1, :]
                        )
                        if t == 4:
                            post = (post_own, post_partner)[(i - ROWS) // ROWS]
                            for f in range(2):
                                post[f, stored(i % ROWS), at, :] = levels[4][i][f][:, :width]
            return carry

        lax.fori_loop(0, SLAB // 8, group, 0)


def stencil(width, own, rx, ry, rxy, p1, p2, inner, kap, spread, factor):
    return pl.pallas_call(
        functools.partial(stencil_kernel, width),
        out_shape=[jax.ShapeDtypeStruct((2, ROWS, 2 * SLAB, width), jnp.float32)] * 2,
        in_specs=[pl.BlockSpec(memory_space=pltpu.VMEM)] * 8
        + [pl.BlockSpec(memory_space=pltpu.SMEM)] * 2,
        out_specs=[pl.BlockSpec(memory_space=pltpu.VMEM)] * 2,
        scratch_shapes=[pltpu.VMEM((2, COUNT, width + 128), jnp.float32)],
        compiler_params=params(),
        cost_estimate=cost(1 << 24, 4 << 20),
        name="outer_substeps",
    )(own, rx, ry, rxy, p1, p2, inner, kap, spread, factor)


def split(values):
    high = values.astype(jnp.bfloat16)
    return high, (values - high.astype(jnp.float32)).astype(jnp.bfloat16)


def solve_kernel(*refs):
    mine, other, (stack_w, stack_h, km), blocks = refs[:2], refs[2:4], refs[4:7], refs[7:]
    dot = functools.partial(jnp.dot, preferred_element_type=jnp.float32)
    half = 2 * SLAB

    def apply(stack, values):
        high, low = split(values)
        count = stack.shape[0] // 2
        both = dot(stack[...], high)
        return both[:count] + both[count:] + dot(stack[:count, :], low)

    for r in range(2 * ROWS):
        strip, inner = divmod(r, ROWS)
        heat = apply(stack_h, jnp.concatenate([mine[strip][0, inner], other[strip][0, inner]], axis=0))
        wet = apply(stack_w, jnp.concatenate([mine[strip][1, inner], other[strip][1, inner]], axis=0))
        factor = km[r : r + 1, :]
        results = (
            heat + factor * wet[half : 2 * half],
            wet[:half] + factor * wet[2 * half :],
        )
        for f in range(2):
            base = (f * ROWS + inner) * SLAB
            for slab in range(2):
                blocks[2 * strip + slab][base : base + SLAB, :] = results[f][
                    slab * SLAB : slab * SLAB + SLAB
                ]


def solve(width, mine, other, stack_w, stack_h, km):
    shape = jax.ShapeDtypeStruct((BODY, width), jnp.float32)
    return pl.pallas_call(
        solve_kernel,
        out_shape=[shape] * 4,
        in_specs=[pl.BlockSpec(memory_space=pltpu.VMEM)] * 7,
        out_specs=[pl.BlockSpec(memory_space=pltpu.VMEM)] * 4,
        compiler_params=params(),
        cost_estimate=cost(1 << 26, 4 << 20),
        name="solve",
    )(*mine, *other, stack_w, stack_h, km)


def assemble_kernel(k, width, *refs):
    blocks, outs, scratch, sems = refs[:4], refs[-4:-2], refs[-2], refs[-1]
    columns = outs[0].shape[2]
    copies = []
    for mask in range(4):
        start = column_start(k, mask, columns)
        for f in range(2):
            for r in range(ROWS):
                base = (f * ROWS + r) * SLAB
                scratch[mask, f, :, r, :] = blocks[mask][base : base + SLAB, :]
            copy = pltpu.make_async_copy(
                scratch.at[mask, f],
                outs[f].at[:, :, pl.ds(start, width)],
                sems.at[2 * mask + f],
            )
            copy.start()
            copies.append(copy)
    for copy in copies:
        copy.wait()


def assemble(k, width, columns, blocks, outs, tail):
    shape = jax.ShapeDtypeStruct((SLAB, ROWS, columns), jnp.float32)
    return pl.pallas_call(
        functools.partial(assemble_kernel, k, width),
        out_shape=[shape] * 2,
        in_specs=[pl.BlockSpec(memory_space=pltpu.VMEM)] * 4
        + [pl.BlockSpec(memory_space=pltpu.HBM)] * len(outs)
        + [pl.BlockSpec(memory_space=pl.ANY)] * len(tail),
        out_specs=[pl.BlockSpec(memory_space=pltpu.HBM)] * 2,
        scratch_shapes=[
            pltpu.VMEM((4, 2, SLAB, ROWS, width), jnp.float32),
            pltpu.SemaphoreType.DMA((8,)),
        ],
        input_output_aliases={4 + i: i for i in range(len(outs))},
        compiler_params=params(),
        cost_estimate=cost(0, 4 << 20),
        name="assemble",
    )(*blocks, *outs, *tail)


def routes(strips):
    cells = [(l, d) for l in range(strips) for d in range(4)]

    def pairs(to):
        return [
            (l * 4 + d, to(l, d)[0] * 4 + to(l, d)[1])
            for l, d in cells
            if 0 <= to(l, d)[0] < strips
        ]

    return {
        "x": pairs(lambda l, d: (l, d ^ 2)),
        "y": pairs(lambda l, d: (l ^ 1, d)),
        "xy": pairs(lambda l, d: (l ^ 1, d ^ 2)),
        "core": pairs(lambda l, d: (l, d ^ 1)),
        "own": pairs(lambda l, d: (l + 2 if l % 2 else l - 2, d)),
        "partner": pairs(lambda l, d: (l - 2 if l % 2 else l + 2, d)),
    }


def per_device(strips, heat, wet, label, spread, factor, thermal, water):
    columns = heat.shape[2]
    widths = [chunk_width(k, columns) for k in range(len(PARTS))]
    route = routes(strips)

    def send(array, name):
        return lax.ppermute(array, JOINT, route[name])

    received = []
    for k, width in enumerate(widths):
        own, bx, by, bxy = pack(k, width, heat, wet, label)
        if k:
            bxy = lax.optimization_barrier((bxy, received[k - 1][2]))[0]
        received.append((own, send(bx, "x"), send(by, "y"), send(bxy, "xy")))
    stack_w, stack_h = prep(thermal, water)
    outs = []
    before, tail = None, []

    def after(value, *others):
        return lax.optimization_barrier((value, *others))[0] if others else value

    for k, width in enumerate(widths):
        own, rx, ry, rxy = received[k]
        if k:
            ry = after(ry, before[1])
            hop = send(jnp.concatenate([rx, ry, rxy, own])[:HOP_ROWS], "core")
        p1 = send(jnp.stack([own, rx]), "own")
        p2 = send(jnp.stack([ry, rxy]), "partner")
        inner, kap, km = pre(width, own, rx, ry, rxy, spread, factor, hop if k else stack_h)
        if k:
            kap = after(kap, before[0])
        mine = stencil(width, own, rx, ry, rxy, p1, p2, inner, kap, spread, factor)
        other = [send(piece, "core") for piece in mine]
        kept, bx, by, bxy = solve(width, mine, other, stack_w, stack_h, km)
        arrived = [send(bx, "x"), send(by, "y"), send(bxy, "xy")]
        before = (kept, km)
        outs = assemble(k, width, columns, [kept, *arrived], outs, tail)
        if k + 1 < len(widths):
            tail = [send(jnp.concatenate([block[:TAIL_ROWS] for block in arrived]), "core")]
        else:
            tail = []
    return tuple(outs)


def solution(mesh):
    return jax.shard_map(
        functools.partial(per_device, mesh.shape["lat"]),
        mesh=mesh,
        in_specs=(
            P("depth", "lat", None),
            P("depth", "lat", None),
            P("lat", None),
            P(),
            P(),
            P(),
            P(),
        ),
        out_specs=(P("depth", "lat", None), P("depth", "lat", None)),
        check_vma=False,
    )
```

```python
import functools

import jax
import jax.numpy as jnp
import numpy as np
from jax import lax
from jax.experimental import pallas as pl
from jax.experimental.pallas import tpu as pltpu
from jax.sharding import PartitionSpec as P

DEPTH = 128
SLAB = 32
ROWS = 4
RATE = 0.25
PARTS = (2, 2)
JOINT = ("lat", "depth")
BODY = 2 * ROWS * SLAB
HOP_ROWS = 816
TAIL_ROWS = 136
VMEM_LIMIT = 48 * 1024 * 1024
FIRST_LIMIT = 62 * 1024 * 1024


def params(limit=VMEM_LIMIT):
    return pltpu.CompilerParams(vmem_limit_bytes=limit)


def cost(flops, nbytes):
    return pl.CostEstimate(flops=0, bytes_accessed=1024, transcendentals=0)


def scaled_cheb(count):
    f32 = np.float32
    index = np.arange(count).astype(f32)
    nodes = np.cos((f32(np.pi) * index / f32(count - 1)).astype(f32)).astype(f32)
    ends = np.where((index == 0) | (index == count - 1), 2.0, 1.0)
    signs = np.where(np.arange(count) % 2 == 0, 1.0, -1.0)
    weight = (ends * signs).astype(f32)
    diagonal = np.eye(count, dtype=bool)
    spread = nodes[:, None] - nodes[None, :]
    off = weight[:, None] / weight[None, :] / np.where(diagonal, f32(1.0), spread)
    off = np.where(diagonal, f32(0.0), off).astype(f32)
    deriv = off - np.diag(np.sum(off, axis=1, dtype=f32))
    scale = (f32(1.0) - nodes * nodes) / f32(count)
    return (scale[:, None] * deriv).astype(f32)


def place():
    lat = lax.axis_index("lat")
    dep = lax.axis_index("depth")
    return lax.rem(lat, 2), lax.div(dep, 2), lax.rem(dep, 2)


def quarter():
    y, x, _ = place()
    return 2 * y + x


def chunk_width(k, columns):
    return columns * PARTS[k] // (4 * sum(PARTS))


def column_start(k, mask, columns):
    width = chunk_width(k, columns)
    place_in_chunk = lax.bitwise_xor(quarter(), mask) * width
    return pl.multiple_of(chunk_start(k, columns) + place_in_chunk, 128)


def chunk_start(k, columns):
    return sum(4 * chunk_width(i, columns) for i in range(k))


def chunk_window(k, columns):
    first = max(chunk_start(k, columns) - 128, 0)
    return first, min(chunk_start(k + 1, columns) + 128, columns)


def halo_at(f, width):
    return (BODY, 128 * f) if width >= 256 else (BODY + 8 * f, 0)


def label_at(width):
    return BODY + (8 if width >= 256 else 16)


def block_rows(width):
    return label_at(width) + 8


def lanes(shape):
    return lax.broadcasted_iota(jnp.int32, shape, len(shape) - 1)


def pack_kernel(k, width, heat_hbm, wet_hbm, label_hbm, *refs):
    *outs, blocks, near, label_ref, sems = refs
    columns = heat_hbm.shape[2]
    first, last = chunk_window(k, columns)
    loads = [
        pltpu.make_async_copy(far.at[:, :, first:last], near.at[f], sems.at[f])
        for f, far in enumerate((heat_hbm, wet_hbm))
    ]
    labels = pltpu.make_async_copy(label_hbm, label_ref, sems.at[2])
    labels.start()
    for load in loads:
        load.start()
    lane = lanes((SLAB, 128))
    lane8 = lanes((8, 128))
    lane4 = lanes((ROWS, 128))

    def window(mask):
        start = column_start(k, mask, columns)
        left = pl.multiple_of(jnp.maximum(start - 128, 0), 128)
        right = pl.multiple_of(jnp.minimum(start + width, columns - 128), 128)
        keep_left = (start > 0).astype(jnp.float32)
        keep_right = (start + width < columns).astype(jnp.float32)
        return start, left, right, keep_left, keep_right

    labels.wait()
    types = label_at(width)
    for mask in range(4):
        start, left, right, keep_left, keep_right = window(mask)
        blocks[mask, types : types + 4, :] = (
            label_ref[:, pl.ds(start, width)] + 1
        ).astype(jnp.float32)
        edge = jnp.where(
            lane4 >= 124,
            (label_ref[:, pl.ds(left, 128)] + 1).astype(jnp.float32) * keep_left,
            (label_ref[:, pl.ds(right, 128)] + 1).astype(jnp.float32) * keep_right,
        )
        blocks[mask, types + 4 : types + 8, :] = jnp.zeros((ROWS, width), jnp.float32)
        blocks[mask, types + 4 : types + 8, :128] = jnp.where(
            (lane4 >= 124) | (lane4 < 4), edge, 0.0
        )
    begin = chunk_start(k, columns)
    here = [lax.bitwise_xor(quarter(), part) for part in range(4)]
    for f in range(2):
        loads[f].wait()
        packed = [jnp.zeros((8, 128), jnp.float32)] * 4
        for r in range(ROWS):
            row = (f * ROWS + r) * SLAB
            tiles = {
                at: near[f, :, r, at - first : at - first + 128]
                for at in range(first, last, 128)
            }
            blank = jnp.zeros((SLAB, 128), jnp.float32)
            for part in range(4):
                start = begin + part * width
                for at in range(start, start + width, 128):
                    blocks[here[part], row : row + SLAB, at - start : at - start + 128] = tiles[at]
                edge = jnp.where(
                    lane >= 64, tiles.get(start - 128, blank), tiles.get(start + width, blank)
                )
                for g in range(SLAB // 8):
                    at = 8 * (r * (SLAB // 8) + g)
                    moved = pltpu.roll(edge[8 * g : 8 * g + 8], (at + 4) % 128, 1)
                    packed[part] = jnp.where((lane8 >= at) & (lane8 < at + 8), moved, packed[part])
        at, lane_at = halo_at(f, width)
        for part in range(4):
            blocks[here[part], at : at + 8, lane_at : lane_at + 128] = packed[part]
    stores = [
        pltpu.make_async_copy(blocks.at[mask], outs[mask], sems.at[3 + mask]) for mask in range(4)
    ]
    for store in stores:
        store.start()
    for store in stores:
        store.wait()


def pack(k, width, heat, wet, label):
    shape = jax.ShapeDtypeStruct((block_rows(width), width), jnp.float32)
    first, last = chunk_window(k, heat.shape[2])
    return pl.pallas_call(
        functools.partial(pack_kernel, k, width),
        out_shape=[shape] * 4,
        in_specs=[pl.BlockSpec(memory_space=pltpu.HBM)] * 3,
        out_specs=[pl.BlockSpec(memory_space=pl.ANY)] * 4,
        scratch_shapes=[
            pltpu.VMEM((4, block_rows(width), width), jnp.float32),
            pltpu.VMEM((2, SLAB, ROWS, last - first), jnp.float32),
            pltpu.VMEM(label.shape, jnp.int32),
            pltpu.SemaphoreType.DMA((7,)),
        ],
        compiler_params=params(VMEM_LIMIT if k else FIRST_LIMIT),
        cost_estimate=cost(0, 4 << 20),
        name="pack",
    )(heat, wet, label)


def prep_kernel(thermal_ref, water_ref, cheb_ref, stack_w_ref, stack_h_ref):
    _, x, c = place()
    dot = functools.partial(
        jnp.dot, precision=lax.Precision.HIGHEST, preferred_element_type=jnp.float32
    )

    def depth_of(n):
        slab, inner = lax.div(n, SLAB), lax.rem(n, SLAB)
        dx = lax.rem(slab, 2)
        dc = lax.div(slab, 2)
        return (2 * lax.rem(x + dx, 2) + lax.rem(c + dc, 2)) * SLAB + inner

    row = lax.broadcasted_iota(jnp.int32, (DEPTH, DEPTH), 0)
    col = lax.broadcasted_iota(jnp.int32, (DEPTH, DEPTH), 1)
    order = (row == depth_of(col)).astype(jnp.float32)
    picks = (depth_of(row[: 2 * SLAB]) == col[: 2 * SLAB]).astype(jnp.float32)
    thermal = dot(picks, thermal_ref[...])
    water = dot(picks, water_ref[...])
    cheb = cheb_ref[...]
    stack_w = jnp.concatenate(
        [water, -0.25 * dot(thermal, cheb), 0.5 * dot(water, cheb)], axis=0
    )
    for ref, stack in ((stack_w_ref, stack_w), (stack_h_ref, thermal)):
        ordered = dot(stack, order)
        high = ordered.astype(jnp.bfloat16)
        low = (ordered - high.astype(jnp.float32)).astype(jnp.bfloat16)
        count = ordered.shape[0]
        ref[:count, :] = high
        ref[count:, :] = low


def prep(thermal, water):
    cheb = jnp.asarray(scaled_cheb(DEPTH))
    return pl.pallas_call(
        prep_kernel,
        out_shape=[
            jax.ShapeDtypeStruct((12 * SLAB, DEPTH), jnp.bfloat16),
            jax.ShapeDtypeStruct((4 * SLAB, DEPTH), jnp.bfloat16),
        ],
        in_specs=[pl.BlockSpec(memory_space=pltpu.VMEM)] * 3,
        out_specs=[pl.BlockSpec(memory_space=pltpu.VMEM)] * 2,
        compiler_params=params(),
        cost_estimate=cost(1 << 24, 1 << 18),
        name="prep",
    )(thermal, water, cheb)


def substep(above, here, below, kappa_heat, kappa_moist):
    laps = []
    size = here[0].shape[1]
    for f in range(2):
        u = here[f]
        sides = pltpu.roll(u, 1, 1) + pltpu.roll(u, size - 1, 1)
        laps.append((above[f] + below[f]) + sides - 4.0 * u)
    heat, wet = here
    body = 1.0 + wet * wet
    guess = pl.reciprocal(body, approx=True)
    inverse = guess * (2.0 - body * guess)
    spread = kappa_heat * (1.5 - 0.5 * inverse)
    return heat + spread * laps[0], wet + kappa_moist * laps[1]


def factors(label, spread_ref, factor_ref):
    heat = jnp.zeros(label.shape, jnp.float32)
    moist = jnp.zeros(label.shape, jnp.float32)
    for i in range(spread_ref.shape[0]):
        here = label == i + 1.0
        heat = jnp.where(here, spread_ref[i], heat)
        moist = jnp.where(here, factor_ref[i], moist)
    return heat, moist


INNER = [(1, 5), (1, 6), (1, 9), (1, 10), (2, 6), (2, 7), (2, 8), (2, 9), (3, 7), (3, 8)]
COUNT = 4 * ROWS


def stored(r):
    return jnp.where(lax.rem(lax.axis_index("lat"), 2) == 1, ROWS - 1 - r, r)


def strip_factors(width, block, spread_ref, factor_ref):
    y, _, _ = place()
    label = block[label_at(width) : label_at(width) + 8, :]
    body = factors(label[:ROWS], spread_ref, factor_ref)
    edge = factors(label[ROWS:, :128], spread_ref, factor_ref)
    for f in range(2):
        whole = jnp.concatenate([body[f], edge[f]], axis=1)
        back = jnp.concatenate([whole[r : r + 1] for r in reversed(range(ROWS))], axis=0)
        yield jnp.where(y == 1, back, whole)


def load_row(width, block, r, g):
    r = stored(r)
    shift = lax.rem(252 - 8 * (r * (SLAB // 8) + g), 128)
    fields = []
    for f in range(2):
        at = pl.multiple_of((f * ROWS + r) * SLAB + 8 * g, 8)
        row, lane = halo_at(f, width)
        edge = pltpu.roll(block[row : row + 8, lane : lane + 128], shift, 1)
        fields.append(jnp.concatenate([block[pl.ds(at, 8), :], edge], axis=1))
    return tuple(fields)


def pre_kernel(width, own, rx, ry, rxy, spread_ref, factor_ref, _, inner, kap, km_ref):
    for j, block in enumerate((own, ry)):
        to = slice(j * ROWS, j * ROWS + ROWS)
        for f, whole in enumerate(strip_factors(width, block, spread_ref, factor_ref)):
            kap[f, to, :] = RATE * whole
            if f == 1:
                km_ref[to, :] = factors(block[label_at(width) : label_at(width) + ROWS, :], spread_ref, factor_ref)[1]
    for s in range(2):
        blocks = ((own, rx)[s], (ry, rxy)[s])

        def group(g, carry):
            levels = [dict() for _ in range(4)]
            at = pl.ds(pl.multiple_of(s * SLAB + 8 * g, 8), 8)
            for j in range(ROWS, 3 * ROWS + 3):
                if j < 3 * ROWS:
                    levels[0][j] = load_row(width, blocks[j // ROWS - 1], j % ROWS, g)
                for t in range(1, 4):
                    i = j - t
                    if ROWS + t <= i < 3 * ROWS - t:
                        prev, k = levels[t - 1], i - ROWS
                        levels[t][i] = substep(
                            prev[i - 1], prev[i], prev[i + 1], kap[0, k : k + 1, :], kap[1, k : k + 1, :]
                        )
                        if (t, i) in INNER:
                            for f in range(2):
                                inner[INNER.index((t, i)), f, at, :] = levels[t][i][f]
            return carry

        lax.fori_loop(0, SLAB // 8, group, 0, unroll=2)


def pre(width, own, rx, ry, rxy, spread, factor, after):
    wide = width + 128
    return pl.pallas_call(
        functools.partial(pre_kernel, width),
        out_shape=[
            jax.ShapeDtypeStruct((len(INNER), 2, 2 * SLAB, wide), jnp.float32),
            jax.ShapeDtypeStruct((2, 2 * ROWS, wide), jnp.float32),
            jax.ShapeDtypeStruct((2 * ROWS, width), jnp.float32),
        ],
        in_specs=[pl.BlockSpec(memory_space=pltpu.VMEM)] * 4
        + [pl.BlockSpec(memory_space=pltpu.SMEM)] * 2
        + [pl.BlockSpec(memory_space=pl.ANY)],
        out_specs=[pl.BlockSpec(memory_space=pltpu.VMEM)] * 3,
        compiler_params=params(),
        cost_estimate=cost(1 << 24, 4 << 20),
        name="inner_substeps",
    )(own, rx, ry, rxy, spread, factor, after)


def stencil_kernel(
    width, own, rx, ry, rxy, p1, p2, inner, kap_ref, spread_ref, factor_ref, post_own, post_partner, kap
):
    kap[:, ROWS : 3 * ROWS, :] = kap_ref[...]
    for j, block in ((0, p2.at[0]), (3, p1.at[0])):
        for f, whole in enumerate(strip_factors(width, block, spread_ref, factor_ref)):
            kap[f, j * ROWS : j * ROWS + ROWS, :] = RATE * whole
    for s in range(2):
        blocks = (p2.at[s], (own, rx)[s], (ry, rxy)[s], p1.at[s])

        def group(g, carry):
            at = pl.ds(pl.multiple_of(s * SLAB + 8 * g, 8), 8)
            levels = [dict() for _ in range(5)]
            for j in range(COUNT + 4):
                if j < COUNT and not ROWS + 2 <= j < 3 * ROWS - 2:
                    levels[0][j] = load_row(width, blocks[j // ROWS], j % ROWS, g)
                for t in range(1, 5):
                    i = j - t
                    if (t, i) in INNER:
                        k = INNER.index((t, i))
                        levels[t][i] = tuple(inner[k, f, at, :] for f in range(2))
                    elif t <= i < COUNT - t and not (t < 4 and ROWS + t <= i < 3 * ROWS - t):
                        prev = levels[t - 1]
                        levels[t][i] = substep(
                            prev[i - 1], prev[i], prev[i + 1], kap[0, i : i + 1, :], kap[1, i : i + 1, :]
                        )
                        if t == 4:
                            post = (post_own, post_partner)[(i - ROWS) // ROWS]
                            for f in range(2):
                                post[f, stored(i % ROWS), at, :] = levels[4][i][f][:, :width]
            return carry

        lax.fori_loop(0, SLAB // 8, group, 0)


def stencil(width, own, rx, ry, rxy, p1, p2, inner, kap, spread, factor):
    return pl.pallas_call(
        functools.partial(stencil_kernel, width),
        out_shape=[jax.ShapeDtypeStruct((2, ROWS, 2 * SLAB, width), jnp.float32)] * 2,
        in_specs=[pl.BlockSpec(memory_space=pltpu.VMEM)] * 8
        + [pl.BlockSpec(memory_space=pltpu.SMEM)] * 2,
        out_specs=[pl.BlockSpec(memory_space=pltpu.VMEM)] * 2,
        scratch_shapes=[pltpu.VMEM((2, COUNT, width + 128), jnp.float32)],
        compiler_params=params(),
        cost_estimate=cost(1 << 24, 4 << 20),
        name="outer_substeps",
    )(own, rx, ry, rxy, p1, p2, inner, kap, spread, factor)


def split(values):
    high = values.astype(jnp.bfloat16)
    return high, (values - high.astype(jnp.float32)).astype(jnp.bfloat16)


def solve_kernel(*refs):
    mine, other, (stack_w, stack_h, km), blocks = refs[:2], refs[2:4], refs[4:7], refs[7:]
    dot = functools.partial(jnp.dot, preferred_element_type=jnp.float32)
    half = 2 * SLAB

    def apply(stack, values):
        high, low = split(values)
        count = stack.shape[0] // 2
        both = dot(stack[...], high)
        return both[:count] + both[count:] + dot(stack[:count, :], low)

    for r in range(2 * ROWS):
        strip, inner = divmod(r, ROWS)
        heat = apply(stack_h, jnp.concatenate([mine[strip][0, inner], other[strip][0, inner]], axis=0))
        wet = apply(stack_w, jnp.concatenate([mine[strip][1, inner], other[strip][1, inner]], axis=0))
        factor = km[r : r + 1, :]
        results = (
            heat + factor * wet[half : 2 * half],
            wet[:half] + factor * wet[2 * half :],
        )
        for f in range(2):
            base = (f * ROWS + inner) * SLAB
            for slab in range(2):
                blocks[2 * strip + slab][base : base + SLAB, :] = results[f][
                    slab * SLAB : slab * SLAB + SLAB
                ]


def solve(width, mine, other, stack_w, stack_h, km):
    shape = jax.ShapeDtypeStruct((BODY, width), jnp.float32)
    return pl.pallas_call(
        solve_kernel,
        out_shape=[shape] * 4,
        in_specs=[pl.BlockSpec(memory_space=pltpu.VMEM)] * 7,
        out_specs=[pl.BlockSpec(memory_space=pltpu.VMEM)] * 4,
        compiler_params=params(),
        cost_estimate=cost(1 << 26, 4 << 20),
        name="solve",
    )(*mine, *other, stack_w, stack_h, km)


def assemble_kernel(k, width, *refs):
    blocks, outs, scratch, sems = refs[:4], refs[-4:-2], refs[-2], refs[-1]
    columns = outs[0].shape[2]
    copies = []
    for mask in range(4):
        start = column_start(k, mask, columns)
        for f in range(2):
            for r in range(ROWS):
                base = (f * ROWS + r) * SLAB
                scratch[mask, f, :, r, :] = blocks[mask][base : base + SLAB, :]
            copy = pltpu.make_async_copy(
                scratch.at[mask, f],
                outs[f].at[:, :, pl.ds(start, width)],
                sems.at[2 * mask + f],
            )
            copy.start()
            copies.append(copy)
    for copy in copies:
        copy.wait()


def assemble(k, width, columns, blocks, outs, tail):
    shape = jax.ShapeDtypeStruct((SLAB, ROWS, columns), jnp.float32)
    return pl.pallas_call(
        functools.partial(assemble_kernel, k, width),
        out_shape=[shape] * 2,
        in_specs=[pl.BlockSpec(memory_space=pltpu.VMEM)] * 4
        + [pl.BlockSpec(memory_space=pltpu.HBM)] * len(outs)
        + [pl.BlockSpec(memory_space=pl.ANY)] * len(tail),
        out_specs=[pl.BlockSpec(memory_space=pltpu.HBM)] * 2,
        scratch_shapes=[
            pltpu.VMEM((4, 2, SLAB, ROWS, width), jnp.float32),
            pltpu.SemaphoreType.DMA((8,)),
        ],
        input_output_aliases={4 + i: i for i in range(len(outs))},
        compiler_params=params(),
        cost_estimate=cost(0, 4 << 20),
        name="assemble",
    )(*blocks, *outs, *tail)


def routes(strips):
    cells = [(l, d) for l in range(strips) for d in range(4)]

    def pairs(to):
        return [
            (l * 4 + d, to(l, d)[0] * 4 + to(l, d)[1])
            for l, d in cells
            if 0 <= to(l, d)[0] < strips
        ]

    return {
        "x": pairs(lambda l, d: (l, d ^ 2)),
        "y": pairs(lambda l, d: (l ^ 1, d)),
        "xy": pairs(lambda l, d: (l ^ 1, d ^ 2)),
        "core": pairs(lambda l, d: (l, d ^ 1)),
        "own": pairs(lambda l, d: (l + 2 if l % 2 else l - 2, d)),
        "partner": pairs(lambda l, d: (l - 2 if l % 2 else l + 2, d)),
    }


def per_device(strips, heat, wet, label, spread, factor, thermal, water):
    columns = heat.shape[2]
    widths = [chunk_width(k, columns) for k in range(len(PARTS))]
    route = routes(strips)

    def send(array, name):
        return lax.ppermute(array, JOINT, route[name])

    received = []
    for k, width in enumerate(widths):
        own, bx, by, bxy = pack(k, width, heat, wet, label)
        if k:
            bxy = lax.optimization_barrier((bxy, received[k - 1][2]))[0]
        received.append((own, send(bx, "x"), send(by, "y"), send(bxy, "xy")))
    stack_w, stack_h = prep(thermal, water)
    outs = []
    before, tail = None, []

    def after(value, *others):
        return lax.optimization_barrier((value, *others))[0] if others else value

    for k, width in enumerate(widths):
        own, rx, ry, rxy = received[k]
        if k:
            ry = after(ry, before[1])
            hop = send(jnp.concatenate([rx, ry, rxy, own])[:HOP_ROWS], "core")
        p1 = send(jnp.stack([own, rx]), "own")
        p2 = send(jnp.stack([ry, rxy]), "partner")
        inner, kap, km = pre(width, own, rx, ry, rxy, spread, factor, hop if k else stack_h)
        if k:
            kap = after(kap, before[0])
        mine = stencil(width, own, rx, ry, rxy, p1, p2, inner, kap, spread, factor)
        other = [send(piece, "core") for piece in mine]
        kept, bx, by, bxy = solve(width, mine, other, stack_w, stack_h, km)
        arrived = [send(bx, "x"), send(by, "y"), send(bxy, "xy")]
        before = (kept, km)
        outs = assemble(k, width, columns, [kept, *arrived], outs, tail)
        if k + 1 < len(widths):
            tail = [send(jnp.concatenate([block[:TAIL_ROWS] for block in arrived]), "core")]
        else:
            tail = []
    return tuple(outs)


def solution(mesh):
    return jax.shard_map(
        functools.partial(per_device, mesh.shape["lat"]),
        mesh=mesh,
        in_specs=(
            P("depth", "lat", None),
            P("depth", "lat", None),
            P("lat", None),
            P(),
            P(),
            P(),
            P(),
        ),
        out_specs=(P("depth", "lat", None), P("depth", "lat", None)),
        check_vma=False,
    )
```

```python
import functools

import jax
import jax.numpy as jnp
import numpy as np
from jax import lax
from jax.experimental import pallas as pl
from jax.experimental.pallas import tpu as pltpu
from jax.sharding import PartitionSpec as P

DEPTH = 128
SLAB = 32
ROWS = 4
RATE = 0.25
PARTS = (2, 2)
JOINT = ("lat", "depth")
BODY = 2 * ROWS * SLAB
HOP_ROWS = 816
TAIL_ROWS = 136
VMEM_LIMIT = 48 * 1024 * 1024
FIRST_LIMIT = 62 * 1024 * 1024


def params(limit=VMEM_LIMIT):
    return pltpu.CompilerParams(vmem_limit_bytes=limit)


def cost(flops, nbytes):
    return pl.CostEstimate(flops=0, bytes_accessed=1024, transcendentals=0)


def scaled_cheb(count):
    f32 = np.float32
    index = np.arange(count).astype(f32)
    nodes = np.cos((f32(np.pi) * index / f32(count - 1)).astype(f32)).astype(f32)
    ends = np.where((index == 0) | (index == count - 1), 2.0, 1.0)
    signs = np.where(np.arange(count) % 2 == 0, 1.0, -1.0)
    weight = (ends * signs).astype(f32)
    diagonal = np.eye(count, dtype=bool)
    spread = nodes[:, None] - nodes[None, :]
    off = weight[:, None] / weight[None, :] / np.where(diagonal, f32(1.0), spread)
    off = np.where(diagonal, f32(0.0), off).astype(f32)
    deriv = off - np.diag(np.sum(off, axis=1, dtype=f32))
    scale = (f32(1.0) - nodes * nodes) / f32(count)
    return (scale[:, None] * deriv).astype(f32)


def place():
    lat = lax.axis_index("lat")
    dep = lax.axis_index("depth")
    return lax.rem(lat, 2), lax.div(dep, 2), lax.rem(dep, 2)


def quarter():
    y, x, _ = place()
    return 2 * y + x


def chunk_width(k, columns):
    return columns * PARTS[k] // (4 * sum(PARTS))


def column_start(k, mask, columns):
    width = chunk_width(k, columns)
    place_in_chunk = lax.bitwise_xor(quarter(), mask) * width
    return pl.multiple_of(chunk_start(k, columns) + place_in_chunk, 128)


def chunk_start(k, columns):
    return sum(4 * chunk_width(i, columns) for i in range(k))


def chunk_window(k, columns):
    first = max(chunk_start(k, columns) - 128, 0)
    return first, min(chunk_start(k + 1, columns) + 128, columns)


def halo_at(f, width):
    return (BODY, 128 * f) if width >= 256 else (BODY + 8 * f, 0)


def label_at(width):
    return BODY + (8 if width >= 256 else 16)


def block_rows(width):
    return label_at(width) + 8


def lanes(shape):
    return lax.broadcasted_iota(jnp.int32, shape, len(shape) - 1)


def pack_kernel(k, width, heat_hbm, wet_hbm, label_hbm, *refs):
    *outs, blocks, near, label_ref, sems = refs
    columns = heat_hbm.shape[2]
    first, last = chunk_window(k, columns)
    loads = [
        pltpu.make_async_copy(far.at[:, :, first:last], near.at[f], sems.at[f])
        for f, far in enumerate((heat_hbm, wet_hbm))
    ]
    labels = pltpu.make_async_copy(label_hbm, label_ref, sems.at[2])
    labels.start()
    for load in loads:
        load.start()
    lane = lanes((SLAB, 128))
    lane8 = lanes((8, 128))
    lane4 = lanes((ROWS, 128))

    def window(mask):
        start = column_start(k, mask, columns)
        left = pl.multiple_of(jnp.maximum(start - 128, 0), 128)
        right = pl.multiple_of(jnp.minimum(start + width, columns - 128), 128)
        keep_left = (start > 0).astype(jnp.float32)
        keep_right = (start + width < columns).astype(jnp.float32)
        return start, left, right, keep_left, keep_right

    labels.wait()
    types = label_at(width)
    for mask in range(4):
        start, left, right, keep_left, keep_right = window(mask)
        blocks[mask, types : types + 4, :] = (
            label_ref[:, pl.ds(start, width)] + 1
        ).astype(jnp.float32)
        edge = jnp.where(
            lane4 >= 124,
            (label_ref[:, pl.ds(left, 128)] + 1).astype(jnp.float32) * keep_left,
            (label_ref[:, pl.ds(right, 128)] + 1).astype(jnp.float32) * keep_right,
        )
        blocks[mask, types + 4 : types + 8, :] = jnp.zeros((ROWS, width), jnp.float32)
        blocks[mask, types + 4 : types + 8, :128] = jnp.where(
            (lane4 >= 124) | (lane4 < 4), edge, 0.0
        )
    begin = chunk_start(k, columns)
    here = [lax.bitwise_xor(quarter(), part) for part in range(4)]
    for f in range(2):
        loads[f].wait()
        packed = [jnp.zeros((8, 128), jnp.float32)] * 4
        for r in range(ROWS):
            row = (f * ROWS + r) * SLAB
            tiles = {
                at: near[f, :, r, at - first : at - first + 128]
                for at in range(first, last, 128)
            }
            blank = jnp.zeros((SLAB, 128), jnp.float32)
            for part in range(4):
                start = begin + part * width
                for at in range(start, start + width, 128):
                    blocks[here[part], row : row + SLAB, at - start : at - start + 128] = tiles[at]
                edge = jnp.where(
                    lane >= 64, tiles.get(start - 128, blank), tiles.get(start + width, blank)
                )
                for g in range(SLAB // 8):
                    at = 8 * (r * (SLAB // 8) + g)
                    moved = pltpu.roll(edge[8 * g : 8 * g + 8], (at + 4) % 128, 1)
                    packed[part] = jnp.where((lane8 >= at) & (lane8 < at + 8), moved, packed[part])
        at, lane_at = halo_at(f, width)
        for part in range(4):
            blocks[here[part], at : at + 8, lane_at : lane_at + 128] = packed[part]
    stores = [
        pltpu.make_async_copy(blocks.at[mask], outs[mask], sems.at[3 + mask]) for mask in range(4)
    ]
    for store in stores:
        store.start()
    for store in stores:
        store.wait()


def pack(k, width, heat, wet, label):
    shape = jax.ShapeDtypeStruct((block_rows(width), width), jnp.float32)
    first, last = chunk_window(k, heat.shape[2])
    return pl.pallas_call(
        functools.partial(pack_kernel, k, width),
        out_shape=[shape] * 4,
        in_specs=[pl.BlockSpec(memory_space=pltpu.HBM)] * 3,
        out_specs=[pl.BlockSpec(memory_space=pl.ANY)] * 4,
        scratch_shapes=[
            pltpu.VMEM((4, block_rows(width), width), jnp.float32),
            pltpu.VMEM((2, SLAB, ROWS, last - first), jnp.float32),
            pltpu.VMEM(label.shape, jnp.int32),
            pltpu.SemaphoreType.DMA((7,)),
        ],
        compiler_params=params(VMEM_LIMIT if k else FIRST_LIMIT),
        cost_estimate=cost(0, 4 << 20),
        name="pack",
    )(heat, wet, label)


def prep_kernel(thermal_ref, water_ref, cheb_ref, stack_w_ref, stack_h_ref):
    _, x, c = place()
    dot = functools.partial(
        jnp.dot, precision=lax.Precision.HIGHEST, preferred_element_type=jnp.float32
    )

    def depth_of(n):
        slab, inner = lax.div(n, SLAB), lax.rem(n, SLAB)
        dx = lax.rem(slab, 2)
        dc = lax.div(slab, 2)
        return (2 * lax.rem(x + dx, 2) + lax.rem(c + dc, 2)) * SLAB + inner

    row = lax.broadcasted_iota(jnp.int32, (DEPTH, DEPTH), 0)
    col = lax.broadcasted_iota(jnp.int32, (DEPTH, DEPTH), 1)
    order = (row == depth_of(col)).astype(jnp.float32)
    picks = (depth_of(row[: 2 * SLAB]) == col[: 2 * SLAB]).astype(jnp.float32)
    thermal = dot(picks, thermal_ref[...])
    water = dot(picks, water_ref[...])
    cheb = cheb_ref[...]
    stack_w = jnp.concatenate(
        [water, -0.25 * dot(thermal, cheb), 0.5 * dot(water, cheb)], axis=0
    )
    for ref, stack in ((stack_w_ref, stack_w), (stack_h_ref, thermal)):
        ordered = dot(stack, order)
        high = ordered.astype(jnp.bfloat16)
        low = (ordered - high.astype(jnp.float32)).astype(jnp.bfloat16)
        count = ordered.shape[0]
        ref[:count, :] = high
        ref[count:, :] = low


def prep(thermal, water):
    cheb = jnp.asarray(scaled_cheb(DEPTH))
    return pl.pallas_call(
        prep_kernel,
        out_shape=[
            jax.ShapeDtypeStruct((12 * SLAB, DEPTH), jnp.bfloat16),
            jax.ShapeDtypeStruct((4 * SLAB, DEPTH), jnp.bfloat16),
        ],
        in_specs=[pl.BlockSpec(memory_space=pltpu.VMEM)] * 3,
        out_specs=[pl.BlockSpec(memory_space=pltpu.VMEM)] * 2,
        compiler_params=params(),
        cost_estimate=cost(1 << 24, 1 << 18),
        name="prep",
    )(thermal, water, cheb)


def substep(above, here, below, kappa_heat, kappa_moist):
    laps = []
    size = here[0].shape[1]
    for f in range(2):
        u = here[f]
        sides = pltpu.roll(u, 1, 1) + pltpu.roll(u, size - 1, 1)
        laps.append((above[f] + below[f]) + sides - 4.0 * u)
    heat, wet = here
    body = 1.0 + wet * wet
    guess = pl.reciprocal(body, approx=True)
    inverse = guess * (2.0 - body * guess)
    spread = kappa_heat * (1.5 - 0.5 * inverse)
    return heat + spread * laps[0], wet + kappa_moist * laps[1]


def factors(label, spread_ref, factor_ref):
    heat = jnp.zeros(label.shape, jnp.float32)
    moist = jnp.zeros(label.shape, jnp.float32)
    for i in range(spread_ref.shape[0]):
        here = label == i + 1.0
        heat = jnp.where(here, spread_ref[i], heat)
        moist = jnp.where(here, factor_ref[i], moist)
    return heat, moist


INNER = [(1, 5), (1, 6), (1, 9), (1, 10), (2, 6), (2, 7), (2, 8), (2, 9), (3, 7), (3, 8)]
COUNT = 4 * ROWS


def stored(r):
    return jnp.where(lax.rem(lax.axis_index("lat"), 2) == 1, ROWS - 1 - r, r)


def strip_factors(width, block, spread_ref, factor_ref):
    y, _, _ = place()
    label = block[label_at(width) : label_at(width) + 8, :]
    body = factors(label[:ROWS], spread_ref, factor_ref)
    edge = factors(label[ROWS:, :128], spread_ref, factor_ref)
    for f in range(2):
        whole = jnp.concatenate([body[f], edge[f]], axis=1)
        back = jnp.concatenate([whole[r : r + 1] for r in reversed(range(ROWS))], axis=0)
        yield jnp.where(y == 1, back, whole)


def load_row(width, block, r, g):
    r = stored(r)
    shift = lax.rem(252 - 8 * (r * (SLAB // 8) + g), 128)
    fields = []
    for f in range(2):
        at = pl.multiple_of((f * ROWS + r) * SLAB + 8 * g, 8)
        row, lane = halo_at(f, width)
        edge = pltpu.roll(block[row : row + 8, lane : lane + 128], shift, 1)
        fields.append(jnp.concatenate([block[pl.ds(at, 8), :], edge], axis=1))
    return tuple(fields)


def pre_kernel(width, own, rx, ry, rxy, spread_ref, factor_ref, _, inner, kap, km_ref):
    for j, block in enumerate((own, ry)):
        to = slice(j * ROWS, j * ROWS + ROWS)
        for f, whole in enumerate(strip_factors(width, block, spread_ref, factor_ref)):
            kap[f, to, :] = RATE * whole
            if f == 1:
                km_ref[to, :] = factors(block[label_at(width) : label_at(width) + ROWS, :], spread_ref, factor_ref)[1]
    for s in range(2):
        blocks = ((own, rx)[s], (ry, rxy)[s])

        def group(g, carry):
            levels = [dict() for _ in range(4)]
            at = pl.ds(pl.multiple_of(s * SLAB + 8 * g, 8), 8)
            for j in range(ROWS, 3 * ROWS + 3):
                if j < 3 * ROWS:
                    levels[0][j] = load_row(width, blocks[j // ROWS - 1], j % ROWS, g)
                for t in range(1, 4):
                    i = j - t
                    if ROWS + t <= i < 3 * ROWS - t:
                        prev, k = levels[t - 1], i - ROWS
                        levels[t][i] = substep(
                            prev[i - 1], prev[i], prev[i + 1], kap[0, k : k + 1, :], kap[1, k : k + 1, :]
                        )
                        if (t, i) in INNER:
                            for f in range(2):
                                inner[INNER.index((t, i)), f, at, :] = levels[t][i][f]
            return carry

        lax.fori_loop(0, SLAB // 8, group, 0, unroll=2)


def pre(width, own, rx, ry, rxy, spread, factor, after):
    wide = width + 128
    return pl.pallas_call(
        functools.partial(pre_kernel, width),
        out_shape=[
            jax.ShapeDtypeStruct((len(INNER), 2, 2 * SLAB, wide), jnp.float32),
            jax.ShapeDtypeStruct((2, 2 * ROWS, wide), jnp.float32),
            jax.ShapeDtypeStruct((2 * ROWS, width), jnp.float32),
        ],
        in_specs=[pl.BlockSpec(memory_space=pltpu.VMEM)] * 4
        + [pl.BlockSpec(memory_space=pltpu.SMEM)] * 2
        + [pl.BlockSpec(memory_space=pl.ANY)],
        out_specs=[pl.BlockSpec(memory_space=pltpu.VMEM)] * 3,
        compiler_params=params(),
        cost_estimate=cost(1 << 24, 4 << 20),
        name="inner_substeps",
    )(own, rx, ry, rxy, spread, factor, after)


def stencil_kernel(
    width, own, rx, ry, rxy, p1, p2, inner, kap_ref, spread_ref, factor_ref, post_own, post_partner, kap
):
    kap[:, ROWS : 3 * ROWS, :] = kap_ref[...]
    for j, block in ((0, p2.at[0]), (3, p1.at[0])):
        for f, whole in enumerate(strip_factors(width, block, spread_ref, factor_ref)):
            kap[f, j * ROWS : j * ROWS + ROWS, :] = RATE * whole
    for s in range(2):
        blocks = (p2.at[s], (own, rx)[s], (ry, rxy)[s], p1.at[s])

        def group(g, carry):
            at = pl.ds(pl.multiple_of(s * SLAB + 8 * g, 8), 8)
            levels = [dict() for _ in range(5)]
            for j in range(COUNT + 4):
                if j < COUNT and not ROWS + 2 <= j < 3 * ROWS - 2:
                    levels[0][j] = load_row(width, blocks[j // ROWS], j % ROWS, g)
                for t in range(1, 5):
                    i = j - t
                    if (t, i) in INNER:
                        k = INNER.index((t, i))
                        levels[t][i] = tuple(inner[k, f, at, :] for f in range(2))
                    elif t <= i < COUNT - t and not (t < 4 and ROWS + t <= i < 3 * ROWS - t):
                        prev = levels[t - 1]
                        levels[t][i] = substep(
                            prev[i - 1], prev[i], prev[i + 1], kap[0, i : i + 1, :], kap[1, i : i + 1, :]
                        )
                        if t == 4:
                            post = (post_own, post_partner)[(i - ROWS) // ROWS]
                            for f in range(2):
                                post[f, stored(i % ROWS), at, :] = levels[4][i][f][:, :width]
            return carry

        lax.fori_loop(0, SLAB // 8, group, 0)


def stencil(width, own, rx, ry, rxy, p1, p2, inner, kap, spread, factor):
    return pl.pallas_call(
        functools.partial(stencil_kernel, width),
        out_shape=[jax.ShapeDtypeStruct((2, ROWS, 2 * SLAB, width), jnp.float32)] * 2,
        in_specs=[pl.BlockSpec(memory_space=pltpu.VMEM)] * 8
        + [pl.BlockSpec(memory_space=pltpu.SMEM)] * 2,
        out_specs=[pl.BlockSpec(memory_space=pltpu.VMEM)] * 2,
        scratch_shapes=[pltpu.VMEM((2, COUNT, width + 128), jnp.float32)],
        compiler_params=params(),
        cost_estimate=cost(1 << 24, 4 << 20),
        name="outer_substeps",
    )(own, rx, ry, rxy, p1, p2, inner, kap, spread, factor)


def split(values):
    high = values.astype(jnp.bfloat16)
    return high, (values - high.astype(jnp.float32)).astype(jnp.bfloat16)


def solve_kernel(*refs):
    mine, other, (stack_w, stack_h, km), blocks = refs[:2], refs[2:4], refs[4:7], refs[7:]
    dot = functools.partial(jnp.dot, preferred_element_type=jnp.float32)
    half = 2 * SLAB

    def apply(stack, values):
        high, low = split(values)
        count = stack.shape[0] // 2
        both = dot(stack[...], high)
        return both[:count] + both[count:] + dot(stack[:count, :], low)

    for r in range(2 * ROWS):
        strip, inner = divmod(r, ROWS)
        heat = apply(stack_h, jnp.concatenate([mine[strip][0, inner], other[strip][0, inner]], axis=0))
        wet = apply(stack_w, jnp.concatenate([mine[strip][1, inner], other[strip][1, inner]], axis=0))
        factor = km[r : r + 1, :]
        results = (
            heat + factor * wet[half : 2 * half],
            wet[:half] + factor * wet[2 * half :],
        )
        for f in range(2):
            base = (f * ROWS + inner) * SLAB
            for slab in range(2):
                blocks[2 * strip + slab][base : base + SLAB, :] = results[f][
                    slab * SLAB : slab * SLAB + SLAB
                ]


def solve(width, mine, other, stack_w, stack_h, km):
    shape = jax.ShapeDtypeStruct((BODY, width), jnp.float32)
    return pl.pallas_call(
        solve_kernel,
        out_shape=[shape] * 4,
        in_specs=[pl.BlockSpec(memory_space=pltpu.VMEM)] * 7,
        out_specs=[pl.BlockSpec(memory_space=pltpu.VMEM)] * 4,
        compiler_params=params(),
        cost_estimate=cost(1 << 26, 4 << 20),
        name="solve",
    )(*mine, *other, stack_w, stack_h, km)


def assemble_kernel(k, width, masks, *refs):
    blocks, outs, scratch, sems = refs[: len(masks)], refs[-4:-2], refs[-2], refs[-1]
    columns = outs[0].shape[2]
    copies = []
    for n, mask in enumerate(masks):
        start = column_start(k, mask, columns)
        for f in range(2):
            for r in range(ROWS):
                base = (f * ROWS + r) * SLAB
                scratch[n, f, :, r, :] = blocks[n][base : base + SLAB, :]
            copy = pltpu.make_async_copy(
                scratch.at[n, f],
                outs[f].at[:, :, pl.ds(start, width)],
                sems.at[2 * n + f],
            )
            copy.start()
            copies.append(copy)
    for copy in copies:
        copy.wait()


def assemble(k, width, columns, masks, blocks, outs, tail):
    shape = jax.ShapeDtypeStruct((SLAB, ROWS, columns), jnp.float32)
    return pl.pallas_call(
        functools.partial(assemble_kernel, k, width, masks),
        out_shape=[shape] * 2,
        in_specs=[pl.BlockSpec(memory_space=pltpu.VMEM)] * len(masks)
        + [pl.BlockSpec(memory_space=pltpu.HBM)] * len(outs)
        + [pl.BlockSpec(memory_space=pl.ANY)] * len(tail),
        out_specs=[pl.BlockSpec(memory_space=pltpu.HBM)] * 2,
        scratch_shapes=[
            pltpu.VMEM((len(masks), 2, SLAB, ROWS, width), jnp.float32),
            pltpu.SemaphoreType.DMA((2 * len(masks),)),
        ],
        input_output_aliases={len(masks) + i: i for i in range(len(outs))},
        compiler_params=params(),
        cost_estimate=cost(0, 4 << 20),
        name="assemble",
    )(*blocks, *outs, *tail)


def routes(strips):
    cells = [(l, d) for l in range(strips) for d in range(4)]

    def pairs(to):
        return [
            (l * 4 + d, to(l, d)[0] * 4 + to(l, d)[1])
            for l, d in cells
            if 0 <= to(l, d)[0] < strips
        ]

    return {
        "x": pairs(lambda l, d: (l, d ^ 2)),
        "y": pairs(lambda l, d: (l ^ 1, d)),
        "xy": pairs(lambda l, d: (l ^ 1, d ^ 2)),
        "core": pairs(lambda l, d: (l, d ^ 1)),
        "own": pairs(lambda l, d: (l + 2 if l % 2 else l - 2, d)),
        "partner": pairs(lambda l, d: (l - 2 if l % 2 else l + 2, d)),
    }


def per_device(strips, heat, wet, label, spread, factor, thermal, water):
    columns = heat.shape[2]
    widths = [chunk_width(k, columns) for k in range(len(PARTS))]
    route = routes(strips)

    def send(array, name):
        return lax.ppermute(array, JOINT, route[name])

    received = []
    for k, width in enumerate(widths):
        own, bx, by, bxy = pack(k, width, heat, wet, label)
        if k:
            bxy = lax.optimization_barrier((bxy, received[k - 1][2]))[0]
        received.append((own, send(bx, "x"), send(by, "y"), send(bxy, "xy")))
    stack_w, stack_h = prep(thermal, water)
    outs = []
    before, tail = None, []

    def after(value, *others):
        return lax.optimization_barrier((value, *others))[0] if others else value

    for k, width in enumerate(widths):
        own, rx, ry, rxy = received[k]
        if k:
            ry = after(ry, before[1])
            hop = send(jnp.concatenate([rx, ry, rxy, own])[:HOP_ROWS], "core")
        p1 = send(jnp.stack([own, rx]), "own")
        p2 = send(jnp.stack([ry, rxy]), "partner")
        inner, kap, km = pre(width, own, rx, ry, rxy, spread, factor, hop if k else stack_h)
        if k:
            kap = after(kap, before[0])
        mine = stencil(width, own, rx, ry, rxy, p1, p2, inner, kap, spread, factor)
        other = [send(piece, "core") for piece in mine]
        kept, bx, by, bxy = solve(width, mine, other, stack_w, stack_h, km)
        arrived = [send(bx, "x"), send(by, "y"), send(bxy, "xy")]
        before = (kept, km)
        if k + 1 < len(widths):
            outs = assemble(k, width, columns, (0, 1, 2, 3), [kept, *arrived], outs, tail)
        else:
            outs = assemble(k, width, columns, (0, 1), [kept, arrived[0]], outs, tail)
            outs = assemble(k, width, columns, (2, 3), arrived[1:], outs, [])
        if k + 1 < len(widths):
            tail = [send(jnp.concatenate([block[:TAIL_ROWS] for block in arrived]), "core")]
        else:
            tail = []
    return tuple(outs)


def solution(mesh):
    return jax.shard_map(
        functools.partial(per_device, mesh.shape["lat"]),
        mesh=mesh,
        in_specs=(
            P("depth", "lat", None),
            P("depth", "lat", None),
            P("lat", None),
            P(),
            P(),
            P(),
            P(),
        ),
        out_specs=(P("depth", "lat", None), P("depth", "lat", None)),
        check_vma=False,
    )
```
